512 devices in a mesh: member: 8 (over y, x_hi), space: 64 (over x_lo, z, core).
Axes of the slice: x: 4 (x_hi: 2, x_lo: 2; x = x_hi * 2 + x_lo), y: 4, z: 16, core: 2. Of those that a mesh axis runs over, the one named last changes fastest.
Arguments:
- latent: bfloat16 [16, 4096, 1024], P('member', 'space'), may hold values from -6 to 6
- edge_weight: float32 [3, 32768], P(None, 'space'), may hold values from 0.1 to 1
- neighbours: int32 [3, 32768], P(None, 'space'), may hold values from 0 to 4095, as said below
- band_rows: int32 [64], P('space'), may hold values from 1 to 512, 24576 in all
- w_in: bfloat16 [1024, 1024], replicated, may hold values from -0.1875 to 0.1875
- w_out: bfloat16 [69, 1024], replicated, may hold values from -0.1875 to 0.1875
- target: float32 [69, 32768], P(None, 'space'), may hold values from -80 to 80
Outputs:
- score: float32 [], replicated
- grad_latent: bfloat16 [16, 4096, 1024], P('member', 'space')
- grad_w_out: float32 [69, 1024], P(None, 'space')
The draws below stay inside these ranges and needn't reach their ends.
Inputs may be any that keep to these rules, and one draw needn't show every extreme that they name: `neighbours`: the node of an edge at grid slot g lies in latitude band g // 512 or one of the two bands beside it, node band b holding nodes b * 64 to (b + 1) * 64 - 1. Band b holds real grid points in its first band_rows[b] slots and padding after them; some band is full.
All inputs are finite; a program needn't handle non-finite values. No bound on the sum of `band_rows` on one device may be relied on, other than what follows from the above.
Results may differ from the reference program's by a relative error of at most 0.0075.
Values may be sent and summed in bfloat16 or wider, within the bound.
No kernel may reach another device: no remote copies, remote signals or barrier semaphores. Data moves between devices by JAX's collectives and lax.ppermute only.
A program may use at most 64 MiB of HBM per device.

```python
import math
import jax
import jax.numpy as jnp
import numpy as np
from jax import lax

D = 1024
VARS = 69
NEIGH = 3
G_DEV = 512
NODE_DEV = 64
MEMBERS = 16
GRID = 32768
NODES = 4096
N_SPACE = 64


def draw_latent(key, part):
    key = jax.random.fold_in(key, 5)
    common_key, cluster_key, sign_key, noise_key, level_key = jax.random.split(key, 5)
    band_count = NODES // NODE_DEV
    common = jax.random.normal(common_key, (1, NODES, D), jnp.float32)
    noise = jax.random.normal(noise_key, (MEMBERS, NODES, D), jnp.float32)
    cluster = jax.random.normal(cluster_key, (1, NODES, D), jnp.float32)
    order = jax.random.permutation(sign_key, jnp.arange(MEMBERS))
    signs = jnp.where(order < MEMBERS // 2, 1.0, -1.0).astype(jnp.float32)[:, None, None]
    levels = jnp.exp(jax.random.uniform(level_key, (MEMBERS, band_count), jnp.float32, -0.5108, 0.47))
    node_band = jnp.arange(NODES) // NODE_DEV
    halves = jnp.where(jnp.arange(NODES) % NODE_DEV < NODE_DEV // 2, 0.3, 1.0).astype(jnp.float32)
    scales = levels[:, node_band] * halves[None, :]
    values = (common + 0.6 * signs * cluster + 0.35 * noise) * scales[:, :, None]
    return jnp.clip(values, -6.0, 6.0).astype(jnp.bfloat16)


def draw_neighbours(key, part):
    band_key, node_key = jax.random.split(jax.random.fold_in(key, 7))
    band_count = GRID // G_DEV
    column_band = jnp.arange(GRID) // G_DEV
    offset = jax.random.randint(band_key, (NEIGH, GRID), -1, 2)
    owner = jnp.clip(column_band[None, :] + offset, 0, band_count - 1)
    half_nodes = NODE_DEV // 2
    picked = jax.random.randint(node_key, (NEIGH, GRID), 0, half_nodes)
    phase = jnp.where(jnp.arange(GRID) % 4 == 0, 0, half_nodes).astype(jnp.int32)
    within = picked + phase[None, :]
    return (owner * NODE_DEV + within).astype(jnp.int32)


def draw_target(key, part):
    heavy_key, scale_key, value_key = jax.random.split(jax.random.fold_in(key, 11), 3)
    band_count = GRID // G_DEV
    heavy = jax.random.randint(heavy_key, (), 0, band_count)
    base = jnp.exp(jax.random.uniform(scale_key, (band_count,), jnp.float32, -0.6931, 0.4055))
    scales = jnp.where(jnp.arange(band_count) == heavy, 25.0, base)
    values = jnp.clip(jax.random.normal(value_key, (VARS, GRID), jnp.float32), -3.0, 3.0)
    return (values * scales[jnp.arange(GRID) // G_DEV][None, :]).astype(jnp.float32)


def block_levels(own_key, extent, cuts, low, largest):
    def one(position, blocks):
        draws = jax.random.uniform(jax.random.fold_in(jax.random.fold_in(own_key, 6), position), (blocks,), jnp.float32, low / len(cuts), largest / len(cuts))
        return jnp.repeat(jnp.exp(draws), extent[position] // blocks).reshape((-1,) + (1,) * (len(extent) - position - 1))

    gain = one(*cuts[0])
    for cut in cuts[1:]:
        gain = gain * one(*cut)
    return gain


def length_profile(amount, total, limit, lean):
    loads = [(1 << 20) // math.isqrt(rank ** lean) + 1 for rank in range(2, amount + 1)]
    surplus, counts = total - limit - (amount - 1), [1] * (amount - 1)
    while surplus > 0:
        free = [i for i in range(amount - 1) if counts[i] < limit]
        mass, remaining = sum([loads[i] for i in free]), surplus
        for i in free:
            extra = min(limit - counts[i], max(1, remaining * loads[i] // mass), surplus)
            counts[i] = counts[i] + extra
            surplus = surplus - extra
    return np.array([limit] + counts)


def uneven(stream_key, number_of, total, most, skew):
    if number_of == 2:
        one = jax.random.randint(stream_key, (), max(1, total - most), min(most, total - 1) + 1)
        return jnp.stack([one, total - one])
    lengths = jnp.asarray(length_profile(number_of, total, most, skew), jnp.int32)
    couples = (number_of - 1) // 2
    giver, receiver = lengths[1:1 + 2 * couples:2], lengths[2:2 + 2 * couples:2]
    room = jnp.minimum(giver - 1, most - receiver)
    passed = jax.random.randint(jax.random.fold_in(stream_key, 1), (couples,), 0, 1 << 20) % (room + 1)
    lengths = lengths.at[1:1 + 2 * couples:2].set(giver - passed).at[2:2 + 2 * couples:2].set(receiver + passed)
    return lengths[jax.random.permutation(jax.random.fold_in(stream_key, 2), number_of)]


def normal_values(rng, shape, scale, most, held_as=jnp.bfloat16):
    result = scale * jax.random.normal(rng, shape, jnp.float32)
    return jnp.clip(result, min=-most, max=most).astype(held_as)


def setup_inputs(seed: int = 0) -> dict:
    streams_of = jax.random.split(jax.random.key(seed), 8)
    return {
        "latent": draw_latent(jax.random.fold_in(streams_of[7], 71), 0),
        "edge_weight": jnp.clip(jnp.exp(math.log(1.0) - 2.3025851 * jax.random.uniform(streams_of[1], (NEIGH, GRID), jnp.float32) ** block_levels(streams_of[1], (NEIGH, GRID), ((1, 64),), -0.2, 0.2)), 0.1, 1.0),
        "neighbours": draw_neighbours(jax.random.fold_in(streams_of[7], 71), 0),
        "band_rows": uneven(streams_of[3], N_SPACE, N_SPACE * G_DEV * 3 // 4, G_DEV, 1).astype(jnp.int32),
        "w_in": normal_values(streams_of[4], (D, D), D ** -0.5, 0.1875),
        "w_out": normal_values(streams_of[5], (VARS, D), D ** -0.5, 0.1875),
        "target": draw_target(jax.random.fold_in(streams_of[7], 71), 0),
    }


epsilon = 1e-06

def partials(everyone, target_rows, valid_rows):
    deviation = everyone - target_rows[None]
    target_sums = lax.optimization_barrier(jnp.sum(valid_rows * deviation * deviation, axis=(1, 2)))

    def against(member_field):
        spread = everyone - member_field[None]
        return lax.optimization_barrier(jnp.sum(valid_rows * spread * spread, axis=(1, 2)))
    pair_sums = lax.map(against, everyone)
    return (target_sums, pair_sums, jnp.sum(valid_rows))

def finish(target_sums, pair_sums, cell_count, variables):
    members = target_sums.shape[0]
    cells = variables * cell_count
    target_dist = jnp.sqrt(target_sums / cells + epsilon)
    pair_dist = jnp.sqrt(pair_sums / cells + epsilon)
    apart = 1.0 - jnp.eye(members, dtype=jnp.float32)
    pair_coef = apart / pair_dist
    score = jnp.mean(target_dist) - jnp.sum(apart * pair_dist) / (2.0 * members * (members - 1))
    return (score, pair_coef, target_dist)

def member_grads(chosen, everyone, coef_rows, dist_rows, target_rows, valid_rows):
    members = everyone.shape[0]
    others = lax.optimization_barrier(jnp.sum(coef_rows[:, :, None, None] * everyone[None], axis=1))
    spread = lax.optimization_barrier(jnp.sum(coef_rows, axis=1))[:, None, None] * chosen - others
    toward = (chosen - target_rows[None]) / (members * dist_rows[:, None, None])
    return (valid_rows * (toward - spread / (members * (members - 1)))).astype(jnp.bfloat16)

def reference(latent, edge_weight, neighbours, band_rows, w_in, w_out, target):
    members = latent.shape[0]
    grid_count = target.shape[1]
    node_count = latent.shape[1]
    latent_width = latent.shape[2]

    def decode(node_latent):
        picked = jnp.take(node_latent, neighbours, axis=0)
        aggregated = edge_weight[0][:, None] * picked[0].astype(jnp.float32)
        for neighbour in range(1, neighbours.shape[0]):
            aggregated = aggregated + edge_weight[neighbour][:, None] * picked[neighbour].astype(jnp.float32)
        latent_mix = aggregated.astype(jnp.bfloat16)
        preact = jnp.dot(latent_mix, w_in, preferred_element_type=jnp.float32)
        hidden = jax.nn.silu(preact).astype(jnp.bfloat16)
        fields = jnp.dot(w_out, hidden.T, preferred_element_type=jnp.float32).astype(jnp.bfloat16)
        return (fields, preact, hidden)
    fields = lax.map(lambda node_latent: decode(node_latent)[0], latent)
    positions = jnp.arange(grid_count)
    valid_rows = (positions % G_DEV < band_rows[positions // G_DEV]).astype(jnp.float32)
    everyone = fields.astype(jnp.float32)
    target_sums, pair_sums, cell_count = partials(everyone, target, valid_rows)
    score, pair_coef, target_dist = finish(target_sums, pair_sums, cell_count, VARS)

    def one_grad(member_index):
        chosen = everyone[member_index][None]
        return member_grads(chosen, everyone, pair_coef[member_index][None], target_dist[member_index][None], target, valid_rows)[0]
    grad_fields = lax.map(one_grad, jnp.arange(members))
    grid_band = (positions // G_DEV).astype(jnp.int32)
    node_band = (neighbours // NODE_DEV).astype(jnp.int32)
    offset = grid_band[None, :] - node_band
    flat_index = neighbours.reshape(-1)

    def node_sum(grad_mixed, which):
        weights = jnp.where(offset == which, edge_weight, 0.0)
        edge_terms = (weights[:, :, None] * grad_mixed[None]).reshape(-1, latent_width)
        return jax.ops.segment_sum(edge_terms, flat_index, num_segments=node_count)

    def backward(carry, inputs):
        node_latent, grad_member = inputs
        unused, preact, hidden = decode(node_latent)
        carry = carry + jnp.dot(grad_member, hidden, preferred_element_type=jnp.float32)
        back = jnp.dot(grad_member.T, w_out, preferred_element_type=jnp.float32)
        sigmoid_part = jax.nn.sigmoid(preact)
        grad_pre = (back * sigmoid_part * (1.0 + preact * (1.0 - sigmoid_part))).astype(jnp.bfloat16)
        grad_mixed = jnp.dot(grad_pre, w_in.T, preferred_element_type=jnp.float32)
        own = node_sum(grad_mixed, 0)
        from_above = lax.optimization_barrier(node_sum(grad_mixed, 1).astype(jnp.bfloat16)).astype(jnp.float32)
        from_below = lax.optimization_barrier(node_sum(grad_mixed, -1).astype(jnp.bfloat16)).astype(jnp.float32)
        node_grad = own + from_above + from_below
        return (carry, node_grad.astype(jnp.bfloat16))
    start_grad = jnp.zeros((w_out.shape[0], latent_width), jnp.float32)
    grad_w_out, grad_latent = lax.scan(backward, start_grad, (latent, grad_fields))
    return (score, grad_latent, grad_w_out)
```

```python
import jax
import jax.numpy as jnp
from jax import lax
from jax.experimental import pallas as pl
from jax.experimental.pallas import tpu as pltpu
from jax.sharding import PartitionSpec as P

epsilon = 1e-06
f32 = jnp.float32
bf16 = jnp.bfloat16
VMEM = pl.BlockSpec(memory_space=pltpu.VMEM)
SMEM = pl.BlockSpec(memory_space=pltpu.SMEM)
NT = (((1,), (1,)), ((), ()))
ROWS = 72
ACROSS = 128


def call(body, outs, specs, scratch=(), limit=24, flops=0, moved=0):
    return pl.pallas_call(
        body,
        out_shape=outs,
        in_specs=specs,
        out_specs=jax.tree.map(lambda _: VMEM, outs),
        scratch_shapes=scratch,
        compiler_params=pltpu.CompilerParams(vmem_limit_bytes=limit << 20),
        cost_estimate=pl.CostEstimate(flops=flops, bytes_accessed=moved, transcendentals=0),
    )


def mixing(neighbours, weight, first_node, rows):
    node = lax.broadcasted_iota(jnp.int32, (rows, neighbours.shape[1]), 0) + first_node
    total = jnp.where(node == neighbours[0:1], weight[0:1], 0.0)
    for k in range(1, neighbours.shape[0]):
        total = total + jnp.where(node == neighbours[k : k + 1], weight[k : k + 1], 0.0)
    return total


def forward(
    place, rows_here, before, own, after, w_in, w_out, neighbours, weight,
    sent, fields, hidden, slope, projected,
):
    members, nodes, _ = before.shape
    slots = neighbours.shape[1]
    step = 128
    first = (place[0] - 1) * nodes
    spread = mixing(neighbours[...], weight[...], first, 4 * nodes).T.astype(bf16)
    for m in range(members):
        projected[m, 0:nodes] = jnp.dot(
            before[m], w_in[...], preferred_element_type=f32
        ).astype(bf16)
        projected[m, nodes : 2 * nodes] = own[m]
        projected[m, 2 * nodes : 3 * nodes] = jnp.dot(
            after[m], w_in[...], preferred_element_type=f32
        ).astype(bf16)
        projected[m, 3 * nodes :] = jnp.zeros_like(own[m])
    slot = lax.broadcasted_iota(jnp.int32, (w_out.shape[0], step), 1)
    for m in range(members):
        for start in range(0, slots, step):
            part = slice(start, start + step)
            preact = jnp.dot(spread[part], projected[m], preferred_element_type=f32)
            gate = 0.5 * jnp.tanh(0.5 * preact) + 0.5
            lit = preact * gate
            out = lit.astype(bf16)
            hidden[m, part] = out
            slope[m, part] = (gate + lit * (1.0 - gate)).astype(bf16)
            decoded = lax.dot_general(w_out[...], out, NT, preferred_element_type=f32)
            fields[m, :, part] = jnp.where(slot + start < rows_here[0], decoded, 0.0).astype(bf16)
    for copy in range(sent.shape[0]):
        sent[copy] = fields[...]


def lanes_of(squares):
    rows, slots = squares.shape
    tall = jnp.sum(squares.reshape(rows // 8, 8, slots), axis=0)
    total = tall[:, 0:128]
    for start in range(128, slots, 128):
        total = total + tall[:, start : start + 128]
    return jnp.sum(total, axis=0, keepdims=True)


def distances(rows_here, everyone, mine, target, sums):
    members = everyone.shape[0]
    lines = []
    for a in range(mine.shape[0]):
        own = mine[a].astype(f32)
        for n in range(members):
            gap = own - everyone[n].astype(f32)
            lines.append(lanes_of(gap * gap))
    for a in range(mine.shape[0]):
        gap = mine[a].astype(f32) - target[...]
        lines.append(lanes_of(gap * gap))
    lines.append(jnp.zeros((128 - len(lines), 128), f32))
    table = jnp.concatenate(lines, axis=0).T
    line = jnp.sum(table, axis=0, keepdims=True)
    lane = lax.broadcasted_iota(jnp.int32, (1, 128), 1)
    line = jnp.where(lane == 127, rows_here[0].astype(f32), line)
    sums[...] = jnp.broadcast_to(line, sums.shape)


def output_grads(variables, place, sums, everyone, mine, target, hidden, grads, weight_grad, share):
    members = everyone.shape[0]
    held = mine.shape[0]
    line = jnp.sum(sums[...], axis=0, keepdims=True)
    lane = lax.broadcasted_iota(jnp.int32, (1, 128), 1)
    cells = variables * line[:, 127:128]
    dist = jnp.sqrt(line / cells + epsilon)
    pairs = held * members
    apart = lane < pairs
    for a in range(held):
        apart = apart & (lane != a * members + place[0] + a)
    coef = jnp.where(apart, 1.0 / dist, 0.0)
    per_target = (lane >= pairs) & (lane < pairs + held)
    share[...] = jnp.sum(
        jnp.where(per_target, dist / members, 0.0)
        - jnp.where(apart, dist / (2.0 * members * (members - 1)), 0.0),
        axis=1, keepdims=True,
    ) + jnp.zeros(share.shape, f32)
    total = None
    for a in range(held):
        chosen = mine[a].astype(f32)
        first = a * members
        reach = jnp.sum(jnp.where((lane >= first) & (lane < first + members), coef, 0.0), axis=1, keepdims=True)
        others = coef[:, first : first + 1] * everyone[0].astype(f32)
        for n in range(1, members):
            others = others + coef[:, first + n : first + n + 1] * everyone[n].astype(f32)
        toward = (chosen - target[...]) * (1.0 / (members * dist[:, pairs + a : pairs + a + 1]))
        grad = (toward - (reach * chosen - others) * (1.0 / (members * (members - 1)))).astype(bf16)
        grads[a] = grad
        part = jnp.dot(grad, hidden[a], preferred_element_type=f32)
        total = part if total is None else total + part
    tall = jnp.concatenate([total, jnp.zeros((ACROSS - total.shape[0], total.shape[1]), f32)], axis=0)
    weight_grad[...] = tall.T.astype(bf16).reshape(weight_grad.shape)


def backward(place, grads, w_out, slope, neighbours, weight, below, middle, above):
    held, nodes, _ = middle.shape
    first = (place[0] - 1) * nodes
    slots = neighbours.shape[1]
    step = 128
    spread = mixing(neighbours[...], weight[...], first, 3 * nodes).astype(bf16)
    for m in range(held):
        total = None
        lines = grads[m].astype(f32).T.astype(bf16)
        for start in range(0, slots, step):
            part = slice(start, start + step)
            back = jnp.dot(lines[part], w_out[...], preferred_element_type=f32)
            grad_pre = (back * slope[m, part].astype(f32)).astype(bf16)
            term = jnp.dot(spread[:, part], grad_pre, preferred_element_type=f32)
            total = term if total is None else total + term
        below[m] = total[:nodes].astype(bf16)
        middle[m] = total[nodes : 2 * nodes]
        above[m] = total[2 * nodes :].astype(bf16)


def node_grads(middle, from_above, from_below, w_in, out):
    for m in range(out.shape[0]):
        total = middle[m] + from_above[m].astype(f32) + from_below[m].astype(f32)
        out[m] = lax.dot_general(
            total.astype(bf16), w_in[...], NT, preferred_element_type=f32
        ).astype(bf16)


def gathered_sum(parts, share, out):
    total = jnp.sum(parts[...].astype(f32), axis=0)
    lane = lax.broadcasted_iota(jnp.int32, total.shape, 1)
    total = jnp.where(lane == ACROSS - 1, share[0:1, 0:1], total)
    out[...] = jnp.broadcast_to(total[None], out.shape)


def last_sum(parts, weight_grad, score):
    total = parts[0]
    for k in range(1, parts.shape[0]):
        total = total + parts[k]
    short = max(128 - total.shape[0], 0)
    tall = jnp.pad(total, ((0, short), (0, 0)))
    weight_grad[...] = tall.T[: weight_grad.shape[0], : weight_grad.shape[1]]
    score[...] = total[0:1, ACROSS - 1 :]


def per_device(latent, edge_weight, neighbours, band_rows, w_in, w_out, target):
    members_dev, nodes, width = latent.shape
    slots = edge_weight.shape[1]
    variables = w_out.shape[0]
    groups, bands = lax.axis_size("member"), lax.axis_size("space")
    members = groups * members_dev
    band = lax.axis_index("space").astype(jnp.int32)
    group = lax.axis_index("member").astype(jnp.int32)
    up = [(i, i + 1) for i in range(bands - 1)]
    down = [(i + 1, i) for i in range(bands - 1)]
    before = lax.ppermute(latent, "space", up)
    after = lax.ppermute(latent, "space", down)
    own = jnp.dot(
        latent.reshape(members_dev * nodes, width), w_in, preferred_element_type=f32
    ).astype(bf16).reshape(latent.shape)
    w_rows = jnp.pad(w_out, ((0, ROWS - variables), (0, 0)))
    real = jnp.arange(slots) < band_rows[0]
    masked = jnp.where(real[None], jnp.pad(target, ((0, ROWS - variables), (0, 0))), 0.0)
    where = band.reshape(1)

    shape = jax.ShapeDtypeStruct
    big = (members_dev, slots, width)
    decoded = (members_dev, ROWS, slots)
    sent, fields, hidden, slope = call(
        forward,
        (shape((groups, *decoded), bf16), shape(decoded, bf16), shape(big, bf16), shape(big, bf16)),
        [SMEM, SMEM] + [VMEM] * 7,
        [pltpu.VMEM((members_dev, 4 * nodes, width), bf16)],
        limit=32, flops=1 << 30, moved=8 << 20,
    )(where, band_rows, before, own, after, w_in, w_rows, neighbours, edge_weight)

    everyone = lax.all_to_all(sent, "member", 0, 0, tiled=True).reshape(members, ROWS, slots)
    mine_at = group * members_dev

    sums = call(
        distances, shape((bands, 128), f32), [SMEM] + [VMEM] * 3, flops=1 << 22, moved=2 << 20
    )(band_rows, everyone, fields, masked)
    sums = lax.all_to_all(sums, "space", 0, 0, tiled=True)

    columns = width // bands

    def grads_body(*refs):
        output_grads(variables, *refs)

    grads, weight_parts, share = call(
        grads_body,
        (shape(decoded, bf16), shape((bands, columns, ACROSS), bf16), shape((8, 128), f32)),
        [SMEM] + [VMEM] * 5, flops=1 << 28, moved=4 << 20,
    )(mine_at.reshape(1), sums, everyone, fields, masked, hidden)
    weight_parts = lax.all_to_all(weight_parts, "space", 0, 0, tiled=True)

    small = (members_dev, nodes, width)
    lower, middle, upper = call(
        backward,
        (shape(small, bf16), shape(small, f32), shape(small, bf16)),
        [SMEM] + [VMEM] * 5, flops=1 << 29, moved=4 << 20,
    )(where, grads, w_rows, slope, neighbours, edge_weight)
    from_above = lax.ppermute(lower, "space", down)
    from_below = lax.ppermute(upper, "space", up)
    grad_latent = call(
        node_grads, shape(small, bf16), [VMEM] * 4, flops=1 << 28, moved=4 << 20
    )(middle, from_above, from_below, w_in)

    total = call(
        gathered_sum, shape((groups, columns, ACROSS), f32), [VMEM] * 2, flops=1 << 18, moved=1 << 18
    )(weight_parts, share)
    total = lax.all_to_all(total, "member", 0, 0, tiled=True)
    grad_w_out, score = call(
        last_sum, (shape((variables, columns), f32), shape((1, 1), f32)), [VMEM], flops=1 << 16, moved=1 << 16
    )(total)
    return (score.reshape(()), grad_latent, grad_w_out)


def solution(mesh):
    return jax.shard_map(
        per_device,
        mesh=mesh,
        in_specs=(
            P("member", "space", None),
            P(None, "space"),
            P(None, "space"),
            P("space"),
            P(),
            P(),
            P(None, "space"),
        ),
        out_specs=(P(), P("member", "space", None), P(None, "space")),
        check_vma=False,
    )
```

```python
import jax
import jax.numpy as jnp
from jax import lax
from jax.experimental import pallas as pl
from jax.experimental.pallas import tpu as pltpu
from jax.sharding import PartitionSpec as P

epsilon = 1e-06
f32 = jnp.float32
bf16 = jnp.bfloat16
VMEM = pl.BlockSpec(memory_space=pltpu.VMEM)
SMEM = pl.BlockSpec(memory_space=pltpu.SMEM)
NT = (((1,), (1,)), ((), ()))
ROWS = 72
ACROSS = 128


HBM = pl.BlockSpec(memory_space=pltpu.HBM)


def call(body, outs, specs, out_specs, scratch=(), room=24 << 10, flops=0, moved=0):
    return pl.pallas_call(
        body,
        out_shape=outs,
        in_specs=specs,
        out_specs=out_specs,
        scratch_shapes=scratch,
        compiler_params=pltpu.CompilerParams(vmem_limit_bytes=room << 10),
        cost_estimate=pl.CostEstimate(flops=flops, bytes_accessed=moved, transcendentals=0),
    )


def mixing(neighbours, weight, first_node, rows):
    node = lax.broadcasted_iota(jnp.int32, (rows, neighbours.shape[1]), 0) + first_node
    total = jnp.where(node == neighbours[0:1], weight[0:1], 0.0)
    for k in range(1, neighbours.shape[0]):
        total = total + jnp.where(node == neighbours[k : k + 1], weight[k : k + 1], 0.0)
    return total


def forward(
    place, rows_here, before, own, after, w_in, w_out, neighbours, weight,
    sent, hidden, slope,
    weights, latents, projected, w_rows, decoded, lit_held, slope_held, w_sems, lit_sems, slope_sems, sent_sems,
):
    members, nodes, width = own.shape
    slots = neighbours.shape[1]
    loads = []
    pieces = w_sems.shape[0]
    for index in range(pieces):
        part = slice(index * (width // pieces), (index + 1) * (width // pieces))
        load = pltpu.make_async_copy(w_in.at[part], weights.at[part], w_sems.at[index])
        load.start()
        loads.append(load)
    step = 128
    first = (place[0] - 1) * nodes
    around = 3 * nodes
    spread = mixing(neighbours[...], weight[...], first, around)
    spread = jnp.concatenate([spread, spread], axis=0).T.astype(bf16)
    for m in range(members):
        for k, source in enumerate((before, own, after)):
            latents[m * around + k * nodes : m * around + (k + 1) * nodes] = source[m]
    for load in loads:
        load.wait()
    whole = jnp.dot(latents[...], weights[...], preferred_element_type=f32)
    high = whole.astype(bf16)
    low = (whole - high.astype(f32)).astype(bf16)
    for m in range(members):
        projected[m, :around] = high[m * around : (m + 1) * around]
        projected[m, around:] = low[m * around : (m + 1) * around]
    variables = w_out.shape[0]
    w_rows[64:ROWS] = jnp.zeros((ROWS - 64, width), f32)
    w_rows[0:variables] = w_out[...].astype(f32)
    rows = w_rows[...].astype(bf16)
    slot = lax.broadcasted_iota(jnp.int32, (ROWS, step), 1)
    copies = []
    for m in range(members):
        for index, start in enumerate(range(0, slots, step)):
            part = slice(start, start + step)
            preact = jnp.dot(spread[part], projected[m], preferred_element_type=f32)
            gate = 0.5 * jnp.tanh(0.5 * preact) + 0.5
            lit = preact * gate
            out = lit.astype(bf16)
            lit_held[m, part] = out
            slope_held[m, part] = (gate + lit * (1.0 - gate)).astype(bf16)
            for held, target, sems in ((lit_held, hidden, lit_sems), (slope_held, slope, slope_sems)):
                copy = pltpu.make_async_copy(held.at[m, part], target.at[m, part], sems.at[m, index])
                copy.start()
                copies.append(copy)
            fields = lax.dot_general(rows, out, NT, preferred_element_type=f32)
            decoded[m, :, part] = jnp.where(slot + start < rows_here[0], fields, 0.0).astype(bf16)
        for k in range(sent.shape[0]):
            copy = pltpu.make_async_copy(decoded.at[m], sent.at[k, m], sent_sems.at[m, k])
            copy.start()
            copies.append(copy)
    for copy in copies:
        copy.wait()


def lanes_of(squares):
    rows, slots = squares.shape
    tall = jnp.sum(squares.reshape(rows // 8, 8, slots), axis=0)
    total = tall[:, 0:128]
    for start in range(128, slots, 128):
        total = total + tall[:, start : start + 128]
    return jnp.sum(total, axis=0, keepdims=True)


def masked_target(rows_here, target, held):
    slot = lax.broadcasted_iota(jnp.int32, target.shape, 1)
    held[64:ROWS] = jnp.zeros((ROWS - 64, target.shape[1]), f32)
    held[0 : target.shape[0]] = jnp.where(slot < rows_here[0], target[...], 0.0)


def distances(owned, place, rows_here, everyone, target, sums, target_held):
    members = everyone.shape[0]
    masked_target(rows_here, target, target_held)
    lines = []
    for a in range(owned):
        own = everyone[place[0] + a].astype(f32)
        for n in range(members):
            gap = own - everyone[n].astype(f32)
            lines.append(lanes_of(gap * gap))
    for a in range(owned):
        gap = everyone[place[0] + a].astype(f32) - target_held[...]
        lines.append(lanes_of(gap * gap))
    lines.append(jnp.zeros((128 - len(lines), 128), f32))
    table = jnp.concatenate(lines, axis=0).T
    line = jnp.sum(table, axis=0, keepdims=True)
    lane = lax.broadcasted_iota(jnp.int32, (1, 128), 1)
    line = jnp.where(lane == 127, rows_here[0].astype(f32), line)
    sums[...] = jnp.broadcast_to(line, sums.shape)


def output_grads(
    variables, place, rows_here, sums, everyone, target, hidden,
    grads, weight_grad, share,
    target_held, lit, parts_held, lit_sems, parts_sems,
):
    members = everyone.shape[0]
    held = grads.shape[0]
    pieces = lit_sems.shape[1]
    step = lit.shape[1] // pieces
    loads = []
    for a in range(held):
        for index in range(pieces):
            part = slice(index * step, (index + 1) * step)
            load = pltpu.make_async_copy(hidden.at[a, part], lit.at[a, part], lit_sems.at[a, index])
            load.start()
            loads.append(load)
    masked_target(rows_here, target, target_held)
    line = jnp.sum(sums[...], axis=0, keepdims=True)
    lane = lax.broadcasted_iota(jnp.int32, (1, 128), 1)
    cells = variables * line[:, 127:128]
    dist = jnp.sqrt(line / cells + epsilon)
    pairs = held * members
    apart = lane < pairs
    for a in range(held):
        apart = apart & (lane != a * members + place[0] + a)
    coef = jnp.where(apart, 1.0 / dist, 0.0)
    per_target = (lane >= pairs) & (lane < pairs + held)
    share[...] = jnp.sum(
        jnp.where(per_target, dist / members, 0.0)
        - jnp.where(apart, dist / (2.0 * members * (members - 1)), 0.0),
        axis=1, keepdims=True,
    ) + jnp.zeros(share.shape, f32)
    shown = []
    for a in range(held):
        chosen = everyone[place[0] + a].astype(f32)
        first = a * members
        reach = jnp.sum(jnp.where((lane >= first) & (lane < first + members), coef, 0.0), axis=1, keepdims=True)
        others = coef[:, first : first + 1] * everyone[0].astype(f32)
        for n in range(1, members):
            others = others + coef[:, first + n : first + n + 1] * everyone[n].astype(f32)
        toward = (chosen - target_held[...]) * (1.0 / (members * dist[:, pairs + a : pairs + a + 1]))
        shown.append((toward - (reach * chosen - others) * (1.0 / (members * (members - 1)))).astype(bf16))
        grads[a] = shown[a]
    for load in loads:
        load.wait()
    total = jnp.dot(shown[0], lit[0], preferred_element_type=f32)
    for a in range(1, held):
        total = total + jnp.dot(shown[a], lit[a], preferred_element_type=f32)
    tall = jnp.concatenate([total, jnp.zeros((ACROSS - total.shape[0], total.shape[1]), f32)], axis=0)
    parts_held[...] = tall.T.astype(bf16).reshape(parts_held.shape)
    pieces = min(parts_sems.shape[0], parts_held.shape[0])
    step = parts_held.shape[0] // pieces
    copies = []
    for index in range(pieces):
        part = slice(index * step, (index + 1) * step)
        copy = pltpu.make_async_copy(parts_held.at[part], weight_grad.at[part], parts_sems.at[index])
        copy.start()
        copies.append(copy)
    for copy in copies:
        copy.wait()


def backward(place, grads, w_out, slope, neighbours, weight, below, middle, above, w_rows):
    held, nodes, width = middle.shape
    variables = w_out.shape[0]
    w_rows[64:ROWS] = jnp.zeros((ROWS - 64, width), f32)
    w_rows[0:variables] = w_out[...].astype(f32)
    rows = w_rows[...].astype(bf16)
    first = (place[0] - 1) * nodes
    slots = neighbours.shape[1]
    step = 128
    spread = mixing(neighbours[...], weight[...], first, 3 * nodes).astype(bf16)
    for m in range(held):
        total = None
        lines = grads[m].astype(f32).T.astype(bf16)
        for start in range(0, slots, step):
            part = slice(start, start + step)
            back = jnp.dot(lines[part], rows, preferred_element_type=f32)
            grad_pre = (back * slope[m, part].astype(f32)).astype(bf16)
            term = jnp.dot(spread[:, part], grad_pre, preferred_element_type=f32)
            total = term if total is None else total + term
        below[m] = total[:nodes].astype(bf16)
        middle[m] = total[nodes : 2 * nodes]
        above[m] = total[2 * nodes :].astype(bf16)


def node_grads(middle, from_above, from_below, w_in, out):
    members, nodes, _ = out.shape
    total = middle[...] + from_above[...].astype(f32) + from_below[...].astype(f32)
    total = total.astype(bf16).reshape(members * nodes, -1)
    done = lax.dot_general(total, w_in[...], NT, preferred_element_type=f32)
    out[...] = done.astype(bf16).reshape(out.shape)


def gathered_sum(parts, share, out):
    total = jnp.sum(parts[...].astype(f32), axis=0)
    lane = lax.broadcasted_iota(jnp.int32, total.shape, 1)
    total = jnp.where(lane == ACROSS - 1, share[0:1, 0:1], total)
    out[...] = jnp.broadcast_to(total[None], out.shape)


def last_sum(parts, weight_grad, score):
    total = parts[0]
    for k in range(1, parts.shape[0]):
        total = total + parts[k]
    weight_grad[...] = total[:, : weight_grad.shape[1]]
    score[...] = total[0:1, ACROSS - 1 :]


def per_device(latent, edge_weight, neighbours, band_rows, w_in, w_out, target):
    members_dev, nodes, width = latent.shape
    slots = edge_weight.shape[1]
    variables = w_out.shape[0]
    groups, bands = lax.axis_size("member"), lax.axis_size("space")
    members = groups * members_dev
    band = lax.axis_index("space").astype(jnp.int32)
    group = lax.axis_index("member").astype(jnp.int32)
    up = [(i, i + 1) for i in range(bands - 1)]
    down = [(i + 1, i) for i in range(bands - 1)]
    before = lax.ppermute(latent, "space", up)
    after = lax.ppermute(latent, "space", down)
    where = band.reshape(1)
    mine_at = (group * members_dev).reshape(1)

    shape = jax.ShapeDtypeStruct
    big = (members_dev, slots, width)
    decoded = (members_dev, ROWS, slots)
    sent, hidden, slope = call(
        forward,
        (shape((groups, *decoded), bf16), shape(big, bf16), shape(big, bf16)),
        [SMEM, SMEM] + [VMEM] * 3 + [HBM] + [VMEM] * 3,
        (HBM, HBM, HBM),
        [
            pltpu.VMEM((width, width), bf16),
            pltpu.VMEM((3 * members_dev * nodes, width), bf16),
            pltpu.VMEM((members_dev, 6 * nodes, width), bf16),
            pltpu.VMEM((ROWS, width), f32),
            pltpu.VMEM(decoded, bf16),
            pltpu.VMEM(big, bf16),
            pltpu.VMEM(big, bf16),
            pltpu.SemaphoreType.DMA((4,)),
            pltpu.SemaphoreType.DMA((members_dev, slots // 128)),
            pltpu.SemaphoreType.DMA((members_dev, slots // 128)),
            pltpu.SemaphoreType.DMA((members_dev, groups)),
        ],
        room=58 << 10, flops=1 << 30, moved=8 << 20,
    )(where, band_rows, before, latent, after, w_in, w_out, neighbours, edge_weight)

    everyone = lax.all_to_all(sent, "member", 0, 0, tiled=True).reshape(members, ROWS, slots)

    def distances_body(*refs):
        distances(members_dev, *refs)

    sums = call(
        distances_body, shape((bands, 128), f32), [SMEM, SMEM, VMEM, VMEM], VMEM,
        [pltpu.VMEM((ROWS, slots), f32)], flops=1 << 22, moved=2 << 20,
    )(mine_at, band_rows, everyone, target)
    sums = lax.all_to_all(sums, "space", 0, 0, tiled=True)

    columns = width // bands
    tiles = (bands, columns, ACROSS)

    def grads_body(*refs):
        output_grads(variables, *refs)

    grads, weight_parts, share = call(
        grads_body,
        (shape(decoded, bf16), shape(tiles, bf16), shape((8, 128), f32)),
        [SMEM, SMEM, VMEM, VMEM, VMEM, HBM],
        (VMEM, HBM, VMEM),
        [
            pltpu.VMEM((ROWS, slots), f32),
            pltpu.VMEM(big, bf16),
            pltpu.VMEM(tiles, bf16),
            pltpu.SemaphoreType.DMA((members_dev, 4)),
            pltpu.SemaphoreType.DMA((4,)),
        ],
        room=60800, flops=1 << 28, moved=4 << 20,
    )(mine_at, band_rows, sums, everyone, target, hidden)
    weight_parts = lax.all_to_all(weight_parts, "space", 0, 0, tiled=True)

    small = (members_dev, nodes, width)
    lower, middle, upper = call(
        backward,
        (shape(small, bf16), shape(small, f32), shape(small, bf16)),
        [SMEM] + [VMEM] * 5,
        (VMEM,) * 3,
        [pltpu.VMEM((ROWS, width), f32)],
        room=60 << 10, flops=1 << 29, moved=4 << 20,
    )(where, grads, w_out, slope, neighbours, edge_weight)
    from_above = lax.ppermute(lower, "space", down)
    from_below = lax.ppermute(upper, "space", up)
    grad_latent = call(
        node_grads, shape(small, bf16), [VMEM] * 4, VMEM, room=58 << 10, flops=1 << 28, moved=4 << 20
    )(middle, from_above, from_below, w_in)

    total = call(
        gathered_sum, shape((groups, columns, ACROSS), f32), [VMEM] * 2, VMEM, flops=1 << 18, moved=1 << 18
    )(weight_parts, share)
    total = lax.all_to_all(total, "member", 0, 0, tiled=True)
    grad_w_out, score = call(
        last_sum, (shape((columns, variables), f32), shape((1, 1), f32)), [VMEM], (VMEM, VMEM),
        flops=1 << 16, moved=1 << 16,
    )(total)
    return (score.reshape(()), grad_latent, grad_w_out.T)


def solution(mesh):
    return jax.shard_map(
        per_device,
        mesh=mesh,
        in_specs=(
            P("member", "space", None),
            P(None, "space"),
            P(None, "space"),
            P("space"),
            P(),
            P(),
            P(None, "space"),
        ),
        out_specs=(P(), P("member", "space", None), P(None, "space")),
        check_vma=False,
    )
```

```python
import jax
import jax.numpy as jnp
from jax import lax
from jax.experimental import pallas as pl
from jax.experimental.pallas import tpu as pltpu
from jax.sharding import PartitionSpec as P

epsilon = 1e-06
f32 = jnp.float32
bf16 = jnp.bfloat16
VMEM = pl.BlockSpec(memory_space=pltpu.VMEM)
SMEM = pl.BlockSpec(memory_space=pltpu.SMEM)
NT = (((1,), (1,)), ((), ()))
ROWS = 72
ACROSS = 128


HBM = pl.BlockSpec(memory_space=pltpu.HBM)


def call(body, outs, specs, out_specs, scratch=(), room=24 << 10, flops=0, moved=0):
    return pl.pallas_call(
        body,
        out_shape=outs,
        in_specs=specs,
        out_specs=out_specs,
        scratch_shapes=scratch,
        compiler_params=pltpu.CompilerParams(vmem_limit_bytes=room << 10),
        cost_estimate=pl.CostEstimate(flops=flops, bytes_accessed=moved, transcendentals=0),
    )


def mixing(neighbours, weight, first_node, rows):
    node = lax.broadcasted_iota(jnp.int32, (rows, neighbours.shape[1]), 0) + first_node
    total = jnp.where(node == neighbours[0:1], weight[0:1], 0.0)
    for k in range(1, neighbours.shape[0]):
        total = total + jnp.where(node == neighbours[k : k + 1], weight[k : k + 1], 0.0)
    return total


def prepare(place, w_in, w_out, neighbours, weight, weights, rows, spread, w_held, w_sems):
    loads = []
    pieces = w_sems.shape[0]
    step = weights.shape[0] // pieces
    for index in range(pieces):
        part = slice(index * step, (index + 1) * step)
        loads.append(pltpu.make_async_copy(w_in.at[part], weights.at[part], w_sems.at[index]))
        loads[-1].start()
    nodes = spread.shape[1] // 6
    mixed = mixing(neighbours[...], weight[...], (place[0] - 1) * nodes, 3 * nodes)
    spread[...] = jnp.concatenate([mixed, mixed], axis=0).T.astype(bf16)
    w_held[64:ROWS] = jnp.zeros((ROWS - 64, w_held.shape[1]), f32)
    w_held[0 : w_out.shape[0]] = w_out[...].astype(f32)
    rows[...] = w_held[...].astype(bf16)
    for load in loads:
        load.wait()


def forward(
    rows_here, before, own, after, weights, rows, spread,
    sent, projected,
    latents, held, decoded, held_sems, sent_sems,
):
    members, nodes, _ = own.shape
    slots = spread.shape[0]
    step = 128
    around = 3 * nodes
    for m in range(members):
        for k, source in enumerate((before, own, after)):
            latents[m * around + k * nodes : m * around + (k + 1) * nodes] = source[m]
    whole = jnp.dot(latents[...], weights[...], preferred_element_type=f32)
    high = whole.astype(bf16)
    low = (whole - high.astype(f32)).astype(bf16)
    copies = []
    for m in range(members):
        held[m, :around] = high[m * around : (m + 1) * around]
        held[m, around:] = low[m * around : (m + 1) * around]
        copies.append(pltpu.make_async_copy(held.at[m], projected.at[m], held_sems.at[m]))
        copies[-1].start()
    slot = lax.broadcasted_iota(jnp.int32, (ROWS, step), 1)
    for m in range(members):
        for start in range(0, slots, step):
            part = slice(start, start + step)
            preact = jnp.dot(spread[part], held[m], preferred_element_type=f32)
            out = (preact * (0.5 * jnp.tanh(0.5 * preact) + 0.5)).astype(bf16)
            fields = lax.dot_general(rows[...], out, NT, preferred_element_type=f32)
            decoded[m, :, part] = jnp.where(slot + start < rows_here[0], fields, 0.0).astype(bf16)
        for k in range(sent.shape[0]):
            copies.append(pltpu.make_async_copy(decoded.at[m], sent.at[k, m], sent_sems.at[m, k]))
            copies[-1].start()
    for copy in copies:
        copy.wait()


def activations(place, projected, neighbours, weight, hidden, slope, held, sems):
    members = projected.shape[0]
    slots = neighbours.shape[1]
    step = 128
    nodes = projected.shape[1] // 6
    spread = mixing(neighbours[...], weight[...], (place[0] - 1) * nodes, 3 * nodes)
    spread = jnp.concatenate([spread, spread], axis=0).T.astype(bf16)
    copies = []
    for m in range(members):
        for index, start in enumerate(range(0, slots, step)):
            part = slice(start, start + step)
            preact = jnp.dot(spread[part], projected[m], preferred_element_type=f32)
            gate = 0.5 * jnp.tanh(0.5 * preact) + 0.5
            lit = preact * gate
            hidden[m, part] = lit.astype(bf16)
            held[m, part] = (gate + lit * (1.0 - gate)).astype(bf16)
            copies.append(pltpu.make_async_copy(held.at[m, part], slope.at[m, part], sems.at[m, index]))
            copies[-1].start()
    for copy in copies:
        copy.wait()


def lanes_of(squares):
    rows, slots = squares.shape
    tall = jnp.sum(squares.reshape(rows // 8, 8, slots), axis=0)
    total = tall[:, 0:128]
    for start in range(128, slots, 128):
        total = total + tall[:, start : start + 128]
    return jnp.sum(total, axis=0, keepdims=True)


def masked_target(rows_here, target, held):
    slot = lax.broadcasted_iota(jnp.int32, target.shape, 1)
    held[64:ROWS] = jnp.zeros((ROWS - 64, target.shape[1]), f32)
    held[0 : target.shape[0]] = jnp.where(slot < rows_here[0], target[...], 0.0)


def distances(owned, place, rows_here, everyone, target, sums, target_held):
    members = everyone.shape[0]
    masked_target(rows_here, target, target_held)
    lines = []
    for a in range(owned):
        own = everyone[place[0] + a].astype(f32)
        for n in range(members):
            gap = own - everyone[n].astype(f32)
            lines.append(lanes_of(gap * gap))
    for a in range(owned):
        gap = everyone[place[0] + a].astype(f32) - target_held[...]
        lines.append(lanes_of(gap * gap))
    lines.append(jnp.zeros((128 - len(lines), 128), f32))
    table = jnp.concatenate(lines, axis=0).T
    line = jnp.sum(table, axis=0, keepdims=True)
    lane = lax.broadcasted_iota(jnp.int32, (1, 128), 1)
    line = jnp.where(lane == 127, rows_here[0].astype(f32), line)
    sums[...] = jnp.broadcast_to(line, sums.shape)


def output_grads(
    variables, place, rows_here, sums, everyone, target, hidden,
    grads, weight_grad, share,
    target_held, shown, parts_held, shown_sems, parts_sems,
):
    members = everyone.shape[0]
    held = grads.shape[0]
    masked_target(rows_here, target, target_held)
    line = jnp.sum(sums[...], axis=0, keepdims=True)
    lane = lax.broadcasted_iota(jnp.int32, (1, 128), 1)
    cells = variables * line[:, 127:128]
    dist = jnp.sqrt(line / cells + epsilon)
    pairs = held * members
    apart = lane < pairs
    for a in range(held):
        apart = apart & (lane != a * members + place[0] + a)
    coef = jnp.where(apart, 1.0 / dist, 0.0)
    per_target = (lane >= pairs) & (lane < pairs + held)
    share[...] = jnp.sum(
        jnp.where(per_target, dist / members, 0.0)
        - jnp.where(apart, dist / (2.0 * members * (members - 1)), 0.0),
        axis=1, keepdims=True,
    ) + jnp.zeros(share.shape, f32)
    copies = []
    for a in range(held):
        chosen = everyone[place[0] + a].astype(f32)
        first = a * members
        reach = jnp.sum(jnp.where((lane >= first) & (lane < first + members), coef, 0.0), axis=1, keepdims=True)
        others = coef[:, first : first + 1] * everyone[0].astype(f32)
        for n in range(1, members):
            others = others + coef[:, first + n : first + n + 1] * everyone[n].astype(f32)
        toward = (chosen - target_held[...]) * (1.0 / (members * dist[:, pairs + a : pairs + a + 1]))
        shown[a] = (toward - (reach * chosen - others) * (1.0 / (members * (members - 1)))).astype(bf16)
        copies.append(pltpu.make_async_copy(shown.at[a], grads.at[a], shown_sems.at[a]))
        copies[-1].start()
    total = jnp.dot(shown[0], hidden[0], preferred_element_type=f32)
    for a in range(1, held):
        total = total + jnp.dot(shown[a], hidden[a], preferred_element_type=f32)
    tall = jnp.concatenate([total, jnp.zeros((ACROSS - total.shape[0], total.shape[1]), f32)], axis=0)
    parts_held[...] = tall.T.astype(bf16).reshape(parts_held.shape)
    pieces = min(parts_sems.shape[0], parts_held.shape[0])
    step = parts_held.shape[0] // pieces
    for index in range(pieces):
        part = slice(index * step, (index + 1) * step)
        copy = pltpu.make_async_copy(parts_held.at[part], weight_grad.at[part], parts_sems.at[index])
        copy.start()
        copies.append(copy)
    for copy in copies:
        copy.wait()


def backward(place, grads, w_out, slope, neighbours, weight, below, middle, above, w_rows):
    held, nodes, width = middle.shape
    variables = w_out.shape[0]
    w_rows[64:ROWS] = jnp.zeros((ROWS - 64, width), f32)
    w_rows[0:variables] = w_out[...].astype(f32)
    rows = w_rows[...].astype(bf16)
    first = (place[0] - 1) * nodes
    slots = neighbours.shape[1]
    step = 128
    spread = mixing(neighbours[...], weight[...], first, 3 * nodes).astype(bf16)
    for m in range(held):
        total = None
        lines = grads[m].astype(f32).T.astype(bf16)
        for start in range(0, slots, step):
            part = slice(start, start + step)
            back = jnp.dot(lines[part], rows, preferred_element_type=f32)
            grad_pre = (back * slope[m, part].astype(f32)).astype(bf16)
            term = jnp.dot(spread[:, part], grad_pre, preferred_element_type=f32)
            total = term if total is None else total + term
        below[m] = total[:nodes].astype(bf16)
        middle[m] = total[nodes : 2 * nodes]
        above[m] = total[2 * nodes :].astype(bf16)


def node_grads(middle, from_above, from_below, w_in, out):
    members, nodes, _ = out.shape
    total = middle[...] + from_above[...].astype(f32) + from_below[...].astype(f32)
    total = total.astype(bf16).reshape(members * nodes, -1)
    done = lax.dot_general(total, w_in[...], NT, preferred_element_type=f32)
    out[...] = done.astype(bf16).reshape(out.shape)


def gathered_sum(parts, share, out):
    total = jnp.sum(parts[...].astype(f32), axis=0)
    lane = lax.broadcasted_iota(jnp.int32, total.shape, 1)
    total = jnp.where(lane == ACROSS - 1, share[0:1, 0:1], total)
    out[...] = jnp.broadcast_to(total[None], out.shape)


def last_sum(parts, weight_grad, score):
    total = parts[0]
    for k in range(1, parts.shape[0]):
        total = total + parts[k]
    weight_grad[...] = total[:, : weight_grad.shape[1]]
    score[...] = total[0:1, ACROSS - 1 :]


def per_device(latent, edge_weight, neighbours, band_rows, w_in, w_out, target):
    members_dev, nodes, width = latent.shape
    slots = edge_weight.shape[1]
    variables = w_out.shape[0]
    groups, bands = lax.axis_size("member"), lax.axis_size("space")
    members = groups * members_dev
    band = lax.axis_index("space").astype(jnp.int32)
    group = lax.axis_index("member").astype(jnp.int32)
    up = [(i, i + 1) for i in range(bands - 1)]
    down = [(i + 1, i) for i in range(bands - 1)]
    before = lax.ppermute(latent, "space", up)
    after = lax.ppermute(latent, "space", down)
    where = band.reshape(1)
    mine_at = (group * members_dev).reshape(1)

    shape = jax.ShapeDtypeStruct
    big = (members_dev, slots, width)
    decoded = (members_dev, ROWS, slots)
    kept = (members_dev, 6 * nodes, width)

    def stay(array):
        return pltpu.with_memory_space_constraint(array, pltpu.HBM)

    weights, rows, spread = call(
        prepare,
        (pltpu.VMEM(w_in.shape, bf16), pltpu.VMEM((ROWS, width), bf16), pltpu.VMEM((slots, 6 * nodes), bf16)),
        [SMEM, HBM] + [VMEM] * 3,
        (VMEM,) * 3,
        [pltpu.VMEM((ROWS, width), f32), pltpu.SemaphoreType.DMA((4,))],
        flops=1 << 22, moved=4 << 20,
    )(where, stay(w_in), stay(w_out), stay(neighbours), stay(edge_weight))
    sent, projected = call(
        forward,
        (pltpu.HBM((groups, *decoded), bf16), pltpu.HBM(kept, bf16)),
        [SMEM] + [VMEM] * 6,
        (HBM, HBM),
        [
            pltpu.VMEM((3 * members_dev * nodes, width), bf16),
            pltpu.VMEM(kept, bf16),
            pltpu.VMEM(decoded, bf16),
            pltpu.SemaphoreType.DMA((members_dev,)),
            pltpu.SemaphoreType.DMA((members_dev, groups)),
        ],
        flops=1 << 30, moved=8 << 20,
    )(band_rows, before, stay(latent), after, weights, rows, spread)

    everyone = lax.all_to_all(sent, "member", 0, 0, tiled=True).reshape(members, ROWS, slots)
    hidden, slope = call(
        activations,
        (pltpu.VMEM(big, bf16), pltpu.HBM(big, bf16)),
        [SMEM] + [VMEM] * 3,
        (VMEM, HBM),
        [pltpu.VMEM(big, bf16), pltpu.SemaphoreType.DMA((members_dev, slots // 128))],
        flops=1 << 30, moved=8 << 20,
    )(where, stay(projected), stay(neighbours), stay(edge_weight))

    def distances_body(*refs):
        distances(members_dev, *refs)

    sums = call(
        distances_body, shape((bands, 128), f32), [SMEM, SMEM, VMEM, VMEM], VMEM,
        [pltpu.VMEM((ROWS, slots), f32)], flops=1 << 22, moved=2 << 20,
    )(mine_at, band_rows, everyone, target)
    sums = lax.all_to_all(sums, "space", 0, 0, tiled=True)

    columns = width // bands
    tiles = (bands, columns, ACROSS)

    def grads_body(*refs):
        output_grads(variables, *refs)

    grads, weight_parts, share = call(
        grads_body,
        (pltpu.HBM(decoded, bf16), pltpu.HBM(tiles, bf16), shape((8, 128), f32)),
        [SMEM, SMEM, VMEM, VMEM, VMEM, VMEM],
        (HBM, HBM, VMEM),
        [
            pltpu.VMEM((ROWS, slots), f32),
            pltpu.VMEM(decoded, bf16),
            pltpu.VMEM(tiles, bf16),
            pltpu.SemaphoreType.DMA((members_dev,)),
            pltpu.SemaphoreType.DMA((4,)),
        ],
        flops=1 << 28, moved=4 << 20,
    )(mine_at, band_rows, sums, everyone, target, hidden)
    weight_parts = lax.all_to_all(weight_parts, "space", 0, 0, tiled=True)

    small = (members_dev, nodes, width)
    lower, middle, upper = call(
        backward,
        (pltpu.VMEM(small, bf16), pltpu.VMEM(small, f32), pltpu.VMEM(small, bf16)),
        [SMEM] + [VMEM] * 5,
        (VMEM,) * 3,
        [pltpu.VMEM((ROWS, width), f32)],
        flops=1 << 29, moved=4 << 20,
    )(where, stay(grads), stay(w_out), stay(slope), stay(neighbours), stay(edge_weight))
    from_above = lax.ppermute(lower, "space", down)
    from_below = lax.ppermute(upper, "space", up)
    grad_latent = call(
        node_grads, shape(small, bf16), [VMEM] * 4, VMEM, flops=1 << 28, moved=4 << 20
    )(middle, from_above, from_below, w_in)

    total = call(
        gathered_sum, shape((groups, columns, ACROSS), f32), [VMEM] * 2, VMEM, flops=1 << 18, moved=1 << 18
    )(weight_parts, share)
    total = lax.all_to_all(total, "member", 0, 0, tiled=True)
    grad_w_out, score = call(
        last_sum, (shape((columns, variables), f32), shape((1, 1), f32)), [VMEM], (VMEM, VMEM),
        flops=1 << 16, moved=1 << 16,
    )(total)
    return (score.reshape(()), grad_latent, grad_w_out.T)


def solution(mesh):
    return jax.shard_map(
        per_device,
        mesh=mesh,
        in_specs=(
            P("member", "space", None),
            P(None, "space"),
            P(None, "space"),
            P("space"),
            P(),
            P(),
            P(None, "space"),
        ),
        out_specs=(P(), P("member", "space", None), P(None, "space")),
        check_vma=False,
    )
```

```python
import jax
import jax.numpy as jnp
from jax import lax
from jax.experimental import pallas as pl
from jax.experimental.pallas import tpu as pltpu
from jax.sharding import PartitionSpec as P

epsilon = 1e-06
f32 = jnp.float32
bf16 = jnp.bfloat16
VMEM = pl.BlockSpec(memory_space=pltpu.VMEM)
SMEM = pl.BlockSpec(memory_space=pltpu.SMEM)
NT = (((1,), (1,)), ((), ()))
ROWS = 72
ACROSS = 128


HBM = pl.BlockSpec(memory_space=pltpu.HBM)


def call(body, outs, specs, out_specs, scratch=(), room=24 << 10, flops=0, moved=0):
    return pl.pallas_call(
        body,
        out_shape=outs,
        in_specs=specs,
        out_specs=out_specs,
        scratch_shapes=scratch,
        compiler_params=pltpu.CompilerParams(vmem_limit_bytes=room << 10),
        cost_estimate=pl.CostEstimate(flops=flops, bytes_accessed=moved, transcendentals=0),
    )


def mixing(neighbours, weight, first_node, rows):
    node = lax.broadcasted_iota(jnp.int32, (rows, neighbours.shape[1]), 0) + first_node
    total = jnp.where(node == neighbours[0:1], weight[0:1], 0.0)
    for k in range(1, neighbours.shape[0]):
        total = total + jnp.where(node == neighbours[k : k + 1], weight[k : k + 1], 0.0)
    return total


def prepare(place, own, w_in, w_out, neighbours, weight, weights, rows, spread, mine, w_held, w_sems):
    loads = []
    pieces = w_sems.shape[0]
    step = weights.shape[0] // pieces
    for index in range(pieces):
        part = slice(index * step, (index + 1) * step)
        loads.append(pltpu.make_async_copy(w_in.at[part], weights.at[part], w_sems.at[index]))
        loads[-1].start()
    nodes = spread.shape[1] // 6
    mixed = mixing(neighbours[...], weight[...], (place[0] - 1) * nodes, 3 * nodes)
    spread[...] = jnp.concatenate([mixed, mixed], axis=0).T.astype(bf16)
    w_held[64:ROWS] = jnp.zeros((ROWS - 64, w_held.shape[1]), f32)
    w_held[0 : w_out.shape[0]] = w_out[...].astype(f32)
    rows[...] = w_held[...].astype(bf16)
    for load in loads:
        load.wait()
    here = own[...].reshape(mine.shape)
    mine[...] = jnp.dot(here, weights[...], preferred_element_type=f32)


def forward(
    rows_here, before, mine, after, weights, rows, spread,
    sent, projected,
    latents, held, decoded, held_sems, sent_sems,
):
    members, nodes, _ = before.shape
    slots = spread.shape[0]
    step = 128
    around = 3 * nodes
    both = members * nodes
    latents[:both] = before[...].reshape(both, -1)
    latents[both:] = after[...].reshape(both, -1)
    whole = jnp.dot(latents[...], weights[...], preferred_element_type=f32)
    for k, source in enumerate((whole[:both], mine[...], whole[both:])):
        high = source.astype(bf16)
        low = (source - high.astype(f32)).astype(bf16)
        for m in range(members):
            first = k * nodes
            held[m, first : first + nodes] = high[m * nodes : (m + 1) * nodes]
            held[m, around + first : around + first + nodes] = low[m * nodes : (m + 1) * nodes]
    copies = []
    for m in range(members):
        copies.append(pltpu.make_async_copy(held.at[m], projected.at[m], held_sems.at[m]))
        copies[-1].start()
    slot = lax.broadcasted_iota(jnp.int32, (ROWS, step), 1)
    for m in range(members):
        for start in range(0, slots, step):
            part = slice(start, start + step)
            preact = jnp.dot(spread[part], held[m], preferred_element_type=f32)
            out = (preact * (0.5 * jnp.tanh(0.5 * preact) + 0.5)).astype(bf16)
            fields = lax.dot_general(rows[...], out, NT, preferred_element_type=f32)
            decoded[m, :, part] = jnp.where(slot + start < rows_here[0], fields, 0.0).astype(bf16)
        for k in range(sent.shape[0]):
            copies.append(pltpu.make_async_copy(decoded.at[m], sent.at[k, m], sent_sems.at[m, k]))
            copies[-1].start()
    for copy in copies:
        copy.wait()


def activations(place, projected, neighbours, weight, hidden, slope, done, held, sems):
    done[...] = jnp.zeros_like(done)
    members = projected.shape[0]
    slots = neighbours.shape[1]
    step = 128
    nodes = projected.shape[1] // 6
    spread = mixing(neighbours[...], weight[...], (place[0] - 1) * nodes, 3 * nodes)
    spread = jnp.concatenate([spread, spread], axis=0).T.astype(bf16)
    copies = []
    for m in range(members):
        for index, start in enumerate(range(0, slots, step)):
            part = slice(start, start + step)
            preact = jnp.dot(spread[part], projected[m], preferred_element_type=f32)
            gate = 0.5 * jnp.tanh(0.5 * preact) + 0.5
            lit = preact * gate
            hidden[m, part] = lit.astype(bf16)
            held[m, part] = (gate + lit * (1.0 - gate)).astype(bf16)
            copies.append(pltpu.make_async_copy(held.at[m, part], slope.at[m, part], sems.at[m, index]))
            copies[-1].start()
    for copy in copies:
        copy.wait()


def lanes_of(squares):
    rows, slots = squares.shape
    tall = jnp.sum(squares.reshape(rows // 8, 8, slots), axis=0)
    total = tall[:, 0:128]
    for start in range(128, slots, 128):
        total = total + tall[:, start : start + 128]
    return jnp.sum(total, axis=0, keepdims=True)


def masked_target(rows_here, target, held):
    slot = lax.broadcasted_iota(jnp.int32, target.shape, 1)
    held[64:ROWS] = jnp.zeros((ROWS - 64, target.shape[1]), f32)
    held[0 : target.shape[0]] = jnp.where(slot < rows_here[0], target[...], 0.0)


def distances(owned, place, rows_here, everyone, target, done, sums, target_held):
    members = everyone.shape[0]
    masked_target(rows_here, target, target_held)
    lines = []
    for a in range(owned):
        own = everyone[place[0] + a].astype(f32)
        for n in range(members):
            gap = own - everyone[n].astype(f32)
            lines.append(lanes_of(gap * gap))
    for a in range(owned):
        gap = everyone[place[0] + a].astype(f32) - target_held[...]
        lines.append(lanes_of(gap * gap))
    lines.append(jnp.zeros((128 - len(lines), 128), f32))
    table = jnp.concatenate(lines, axis=0).T
    line = jnp.sum(table, axis=0, keepdims=True)
    lane = lax.broadcasted_iota(jnp.int32, (1, 128), 1)
    line = jnp.where(lane == 127, rows_here[0].astype(f32), line)
    sums[...] = jnp.broadcast_to(line, sums.shape)


def output_grads(
    variables, place, rows_here, sums, everyone, target, hidden,
    grads, weight_grad, share,
    target_held, shown, parts_held, shown_sems, parts_sems,
):
    members = everyone.shape[0]
    held = grads.shape[0]
    masked_target(rows_here, target, target_held)
    line = jnp.sum(sums[...], axis=0, keepdims=True)
    lane = lax.broadcasted_iota(jnp.int32, (1, 128), 1)
    cells = variables * line[:, 127:128]
    dist = jnp.sqrt(line / cells + epsilon)
    pairs = held * members
    apart = lane < pairs
    for a in range(held):
        apart = apart & (lane != a * members + place[0] + a)
    coef = jnp.where(apart, 1.0 / dist, 0.0)
    per_target = (lane >= pairs) & (lane < pairs + held)
    share[...] = jnp.sum(
        jnp.where(per_target, dist / members, 0.0)
        - jnp.where(apart, dist / (2.0 * members * (members - 1)), 0.0),
        axis=1, keepdims=True,
    ) + jnp.zeros(share.shape, f32)
    copies = []
    for a in range(held):
        chosen = everyone[place[0] + a].astype(f32)
        first = a * members
        reach = jnp.sum(jnp.where((lane >= first) & (lane < first + members), coef, 0.0), axis=1, keepdims=True)
        others = coef[:, first : first + 1] * everyone[0].astype(f32)
        for n in range(1, members):
            others = others + coef[:, first + n : first + n + 1] * everyone[n].astype(f32)
        toward = (chosen - target_held[...]) * (1.0 / (members * dist[:, pairs + a : pairs + a + 1]))
        shown[a] = (toward - (reach * chosen - others) * (1.0 / (members * (members - 1)))).astype(bf16)
        copies.append(pltpu.make_async_copy(shown.at[a], grads.at[a], shown_sems.at[a]))
        copies[-1].start()
    total = jnp.dot(shown[0], hidden[0], preferred_element_type=f32)
    for a in range(1, held):
        total = total + jnp.dot(shown[a], hidden[a], preferred_element_type=f32)
    tall = jnp.concatenate([total, jnp.zeros((ACROSS - total.shape[0], total.shape[1]), f32)], axis=0)
    parts_held[...] = tall.T.astype(bf16).reshape(parts_held.shape)
    pieces = min(parts_sems.shape[0], parts_held.shape[0])
    step = parts_held.shape[0] // pieces
    for index in range(pieces):
        part = slice(index * step, (index + 1) * step)
        copy = pltpu.make_async_copy(parts_held.at[part], weight_grad.at[part], parts_sems.at[index])
        copy.start()
        copies.append(copy)
    for copy in copies:
        copy.wait()


def backward(place, grads, w_out, slope, neighbours, weight, below, middle, above, w_rows):
    held, nodes, width = middle.shape
    variables = w_out.shape[0]
    w_rows[64:ROWS] = jnp.zeros((ROWS - 64, width), f32)
    w_rows[0:variables] = w_out[...].astype(f32)
    rows = w_rows[...].astype(bf16)
    first = (place[0] - 1) * nodes
    slots = neighbours.shape[1]
    step = 128
    spread = mixing(neighbours[...], weight[...], first, 3 * nodes).astype(bf16)
    for m in range(held):
        total = None
        lines = grads[m].astype(f32).T.astype(bf16)
        for start in range(0, slots, step):
            part = slice(start, start + step)
            back = jnp.dot(lines[part], rows, preferred_element_type=f32)
            grad_pre = (back * slope[m, part].astype(f32)).astype(bf16)
            term = jnp.dot(spread[:, part], grad_pre, preferred_element_type=f32)
            total = term if total is None else total + term
        below[m] = total[:nodes].astype(bf16)
        middle[m] = total[nodes : 2 * nodes]
        above[m] = total[2 * nodes :].astype(bf16)


def node_grads(middle, from_above, from_below, w_in, out):
    members, nodes, _ = out.shape
    total = middle[...] + from_above[...].astype(f32) + from_below[...].astype(f32)
    total = total.astype(bf16).reshape(members * nodes, -1)
    done = lax.dot_general(total, w_in[...], NT, preferred_element_type=f32)
    out[...] = done.astype(bf16).reshape(out.shape)


def gathered_sum(parts, share, out):
    total = jnp.sum(parts[...].astype(f32), axis=0)
    lane = lax.broadcasted_iota(jnp.int32, total.shape, 1)
    total = jnp.where(lane == ACROSS - 1, share[0:1, 0:1], total)
    out[...] = jnp.broadcast_to(total[None], out.shape)


def last_sum(parts, weight_grad, score):
    total = parts[0]
    for k in range(1, parts.shape[0]):
        total = total + parts[k]
    weight_grad[...] = total[:, : weight_grad.shape[1]]
    score[...] = total[0:1, ACROSS - 1 :]


def per_device(latent, edge_weight, neighbours, band_rows, w_in, w_out, target):
    members_dev, nodes, width = latent.shape
    slots = edge_weight.shape[1]
    variables = w_out.shape[0]
    groups, bands = lax.axis_size("member"), lax.axis_size("space")
    members = groups * members_dev
    band = lax.axis_index("space").astype(jnp.int32)
    group = lax.axis_index("member").astype(jnp.int32)
    up = [(i, i + 1) for i in range(bands - 1)]
    down = [(i + 1, i) for i in range(bands - 1)]
    before = lax.ppermute(latent, "space", up)
    after = lax.ppermute(latent, "space", down)
    where = band.reshape(1)
    mine_at = (group * members_dev).reshape(1)

    shape = jax.ShapeDtypeStruct
    big = (members_dev, slots, width)
    decoded = (members_dev, ROWS, slots)
    kept = (members_dev, 6 * nodes, width)

    def stay(array):
        return pltpu.with_memory_space_constraint(array, pltpu.HBM)

    weights, rows, spread, mine = call(
        prepare,
        (
            pltpu.VMEM(w_in.shape, bf16), pltpu.VMEM((ROWS, width), bf16),
            pltpu.VMEM((slots, 6 * nodes), bf16), pltpu.VMEM((members_dev * nodes, width), f32),
        ),
        [SMEM, VMEM, HBM] + [VMEM] * 3,
        (VMEM,) * 4,
        [pltpu.VMEM((ROWS, width), f32), pltpu.SemaphoreType.DMA((4,))],
        flops=1 << 28, moved=4 << 20,
    )(where, stay(latent), stay(w_in), stay(w_out), stay(neighbours), stay(edge_weight))
    sent, projected = call(
        forward,
        (pltpu.HBM((groups, *decoded), bf16), pltpu.HBM(kept, bf16)),
        [SMEM] + [VMEM] * 6,
        (HBM, HBM),
        [
            pltpu.VMEM((2 * members_dev * nodes, width), bf16),
            pltpu.VMEM(kept, bf16),
            pltpu.VMEM(decoded, bf16),
            pltpu.SemaphoreType.DMA((members_dev,)),
            pltpu.SemaphoreType.DMA((members_dev, groups)),
        ],
        flops=1 << 30, moved=8 << 20,
    )(band_rows, before, mine, after, weights, rows, spread)

    everyone = lax.all_to_all(sent, "member", 0, 0, tiled=True).reshape(members, ROWS, slots)
    hidden, slope, done = call(
        activations,
        (pltpu.VMEM(big, bf16), pltpu.HBM(big, bf16), shape((8, 128), f32)),
        [SMEM] + [VMEM] * 3,
        (VMEM, HBM, VMEM),
        [pltpu.VMEM(big, bf16), pltpu.SemaphoreType.DMA((members_dev, slots // 128))],
        flops=1 << 30, moved=8 << 20,
    )(where, stay(projected), stay(neighbours), stay(edge_weight))

    def distances_body(*refs):
        distances(members_dev, *refs)

    sums = call(
        distances_body, shape((bands, 128), f32), [SMEM, SMEM, VMEM, VMEM, HBM], VMEM,
        [pltpu.VMEM((ROWS, slots), f32)], flops=1 << 22, moved=2 << 20,
    )(mine_at, band_rows, everyone, target, done)
    sums = lax.all_to_all(sums, "space", 0, 0, tiled=True)

    columns = width // bands
    tiles = (bands, columns, ACROSS)

    def grads_body(*refs):
        output_grads(variables, *refs)

    grads, weight_parts, share = call(
        grads_body,
        (pltpu.HBM(decoded, bf16), pltpu.HBM(tiles, bf16), shape((8, 128), f32)),
        [SMEM, SMEM, VMEM, VMEM, VMEM, VMEM],
        (HBM, HBM, VMEM),
        [
            pltpu.VMEM((ROWS, slots), f32),
            pltpu.VMEM(decoded, bf16),
            pltpu.VMEM(tiles, bf16),
            pltpu.SemaphoreType.DMA((members_dev,)),
            pltpu.SemaphoreType.DMA((4,)),
        ],
        flops=1 << 28, moved=4 << 20,
    )(mine_at, band_rows, sums, everyone, target, hidden)
    weight_parts = lax.all_to_all(weight_parts, "space", 0, 0, tiled=True)

    small = (members_dev, nodes, width)
    lower, middle, upper = call(
        backward,
        (pltpu.VMEM(small, bf16), pltpu.VMEM(small, f32), pltpu.VMEM(small, bf16)),
        [SMEM] + [VMEM] * 5,
        (VMEM,) * 3,
        [pltpu.VMEM((ROWS, width), f32)],
        flops=1 << 29, moved=4 << 20,
    )(where, stay(grads), stay(w_out), stay(slope), stay(neighbours), stay(edge_weight))
    from_above = lax.ppermute(lower, "space", down)
    from_below = lax.ppermute(upper, "space", up)
    grad_latent = call(
        node_grads, shape(small, bf16), [VMEM] * 4, VMEM, flops=1 << 28, moved=4 << 20
    )(middle, from_above, from_below, w_in)

    total = call(
        gathered_sum, shape((groups, columns, ACROSS), f32), [VMEM] * 2, VMEM, flops=1 << 18, moved=1 << 18
    )(weight_parts, share)
    total = lax.all_to_all(total, "member", 0, 0, tiled=True)
    grad_w_out, score = call(
        last_sum, (shape((columns, variables), f32), shape((1, 1), f32)), [VMEM], (VMEM, VMEM),
        flops=1 << 16, moved=1 << 16,
    )(total)
    return (score.reshape(()), grad_latent, grad_w_out.T)


def solution(mesh):
    return jax.shard_map(
        per_device,
        mesh=mesh,
        in_specs=(
            P("member", "space", None),
            P(None, "space"),
            P(None, "space"),
            P("space"),
            P(),
            P(),
            P(None, "space"),
        ),
        out_specs=(P(), P("member", "space", None), P(None, "space")),
        check_vma=False,
    )
```

```python
import jax
import jax.numpy as jnp
from jax import lax
from jax.experimental import pallas as pl
from jax.experimental.pallas import tpu as pltpu
from jax.sharding import PartitionSpec as P

epsilon = 1e-06
f32 = jnp.float32
bf16 = jnp.bfloat16
VMEM = pl.BlockSpec(memory_space=pltpu.VMEM)
SMEM = pl.BlockSpec(memory_space=pltpu.SMEM)
NT = (((1,), (1,)), ((), ()))
ROWS = 72
ACROSS = 128
QUAD = 4


HBM = pl.BlockSpec(memory_space=pltpu.HBM)


def call(body, outs, specs, out_specs, scratch=(), room=24 << 10, flops=0, moved=0):
    return pl.pallas_call(
        body,
        out_shape=outs,
        in_specs=specs,
        out_specs=out_specs,
        scratch_shapes=scratch,
        compiler_params=pltpu.CompilerParams(vmem_limit_bytes=room << 10),
        cost_estimate=pl.CostEstimate(flops=flops, bytes_accessed=moved, transcendentals=0),
    )


def mixing(neighbours, weight, first_node, rows):
    node = lax.broadcasted_iota(jnp.int32, (rows, neighbours.shape[1]), 0) + first_node
    total = jnp.where(node == neighbours[0:1], weight[0:1], 0.0)
    for k in range(1, neighbours.shape[0]):
        total = total + jnp.where(node == neighbours[k : k + 1], weight[k : k + 1], 0.0)
    return total


def prepare(place, own, w_in, w_out, neighbours, weight, weights, rows, spread, mine, w_held, w_sems):
    loads = []
    pieces = w_sems.shape[0]
    step = weights.shape[0] // pieces
    for index in range(pieces):
        part = slice(index * step, (index + 1) * step)
        loads.append(pltpu.make_async_copy(w_in.at[part], weights.at[part], w_sems.at[index]))
        loads[-1].start()
    nodes = spread.shape[1] // 6
    mixed = mixing(neighbours[...], weight[...], (place[0] - 1) * nodes, 3 * nodes)
    spread[...] = jnp.concatenate([mixed, mixed], axis=0).T.astype(bf16)
    w_held[64:ROWS] = jnp.zeros((ROWS - 64, w_held.shape[1]), f32)
    w_held[0 : w_out.shape[0]] = w_out[...].astype(f32)
    rows[...] = w_held[...].astype(bf16)
    for load in loads:
        load.wait()
    here = own[...].reshape(mine.shape)
    mine[...] = jnp.dot(here, weights[...], preferred_element_type=f32)


def forward(
    rows_here, before, mine, after, weights, rows, spread,
    sent, projected,
    latents, held, decoded, held_sems, sent_sems,
):
    members, nodes, _ = before.shape
    slots = spread.shape[0]
    step = 128
    around = 3 * nodes
    both = members * nodes
    latents[:both] = before[...].reshape(both, -1)
    latents[both:] = after[...].reshape(both, -1)
    whole = jnp.dot(latents[...], weights[...], preferred_element_type=f32)
    for k, source in enumerate((whole[:both], mine[...], whole[both:])):
        high = source.astype(bf16)
        low = (source - high.astype(f32)).astype(bf16)
        for m in range(members):
            first = k * nodes
            held[m, first : first + nodes] = high[m * nodes : (m + 1) * nodes]
            held[m, around + first : around + first + nodes] = low[m * nodes : (m + 1) * nodes]
    copies = []
    for m in range(members):
        copies.append(pltpu.make_async_copy(held.at[m], projected.at[m], held_sems.at[m]))
        copies[-1].start()
    slot = lax.broadcasted_iota(jnp.int32, (ROWS, step), 1)
    for m in range(members):
        for start in range(0, slots, step):
            part = slice(start, start + step)
            preact = jnp.dot(spread[part], held[m], preferred_element_type=f32)
            out = (preact * (0.5 * jnp.tanh(0.5 * preact) + 0.5)).astype(bf16)
            fields = lax.dot_general(rows[...], out, NT, preferred_element_type=f32)
            decoded[m, :, part] = jnp.where(slot + start < rows_here[0], fields, 0.0).astype(bf16)
        for k in range(sent.shape[0]):
            copies.append(pltpu.make_async_copy(decoded.at[m], sent.at[k, m], sent_sems.at[m, k]))
            copies[-1].start()
    for copy in copies:
        copy.wait()


def activations(place, projected, neighbours, weight, hidden, slope, done, held, sems):
    done[...] = jnp.zeros_like(done)
    members = projected.shape[0]
    slots = neighbours.shape[1]
    step = 128
    nodes = projected.shape[1] // 6
    spread = mixing(neighbours[...], weight[...], (place[0] - 1) * nodes, 3 * nodes)
    spread = jnp.concatenate([spread, spread], axis=0).T.astype(bf16)
    copies = []
    for m in range(members):
        for index, start in enumerate(range(0, slots, step)):
            part = slice(start, start + step)
            preact = jnp.dot(spread[part], projected[m], preferred_element_type=f32)
            gate = 0.5 * jnp.tanh(0.5 * preact) + 0.5
            lit = preact * gate
            hidden[m, part] = lit.astype(bf16)
            held[m, part] = (gate + lit * (1.0 - gate)).astype(bf16)
            copies.append(pltpu.make_async_copy(held.at[m, part], slope.at[m, part], sems.at[m, index]))
            copies[-1].start()
    for copy in copies:
        copy.wait()


def lanes_of(squares):
    rows, slots = squares.shape
    tall = jnp.sum(squares.reshape(rows // 8, 8, slots), axis=0)
    total = tall[:, 0:128]
    for start in range(128, slots, 128):
        total = total + tall[:, start : start + 128]
    return jnp.sum(total, axis=0, keepdims=True)


def masked_target(rows_here, target, held):
    slot = lax.broadcasted_iota(jnp.int32, target.shape, 1)
    held[64:ROWS] = jnp.zeros((ROWS - 64, target.shape[1]), f32)
    held[0 : target.shape[0]] = jnp.where(slot < rows_here[0], target[...], 0.0)


def distances(owned, place, rows_here, everyone, target, done, sums, target_held):
    members = everyone.shape[0]
    masked_target(rows_here, target, target_held)
    lines = []
    for a in range(owned):
        own = everyone[place[0] + a].astype(f32)
        for n in range(members):
            gap = own - everyone[n].astype(f32)
            lines.append(lanes_of(gap * gap))
    for a in range(owned):
        gap = everyone[place[0] + a].astype(f32) - target_held[...]
        lines.append(lanes_of(gap * gap))
    lines.append(jnp.zeros((128 - len(lines), 128), f32))
    table = jnp.concatenate(lines, axis=0).T
    line = jnp.sum(table, axis=0, keepdims=True)
    lane = lax.broadcasted_iota(jnp.int32, (1, 128), 1)
    line = jnp.where(lane == 127, rows_here[0].astype(f32), line)
    sums[...] = jnp.broadcast_to(line, sums.shape)


def packed(tall):
    rows = tall.shape[0] // QUAD
    column = [tall[pl.ds(k, rows, stride=QUAD), :] for k in range(QUAD)]
    lane = lax.broadcasted_iota(jnp.int32, (rows, ACROSS), 1)
    half = ACROSS // 2
    over = ROWS - half
    rest = pltpu.roll(column[0], half, 1)
    for k in range(1, QUAD):
        rest = jnp.where(lane < k * over, rest, pltpu.roll(column[k], half + k * over, 1))
    return jnp.concatenate(
        [
            jnp.where(lane < half, column[0], pltpu.roll(column[1], half, 1)),
            jnp.where(lane < half, column[2], pltpu.roll(column[3], half, 1)),
            rest,
        ],
        axis=1,
    )


def output_grads(
    variables, place, rows_here, sums, everyone, target, hidden,
    grads, weight_grad, share,
    target_held, shown, tall_held, parts_held, shown_sems, parts_sems,
):
    members = everyone.shape[0]
    held = grads.shape[0]
    masked_target(rows_here, target, target_held)
    line = jnp.sum(sums[...], axis=0, keepdims=True)
    lane = lax.broadcasted_iota(jnp.int32, (1, 128), 1)
    cells = variables * line[:, 127:128]
    dist = jnp.sqrt(line / cells + epsilon)
    pairs = held * members
    apart = lane < pairs
    for a in range(held):
        apart = apart & (lane != a * members + place[0] + a)
    coef = jnp.where(apart, 1.0 / dist, 0.0)
    per_target = (lane >= pairs) & (lane < pairs + held)
    share[...] = jnp.sum(
        jnp.where(per_target, dist / members, 0.0)
        - jnp.where(apart, dist / (2.0 * members * (members - 1)), 0.0),
        axis=1, keepdims=True,
    ) + jnp.zeros(share.shape, f32)
    copies = []
    for a in range(held):
        chosen = everyone[place[0] + a].astype(f32)
        first = a * members
        reach = jnp.sum(jnp.where((lane >= first) & (lane < first + members), coef, 0.0), axis=1, keepdims=True)
        others = coef[:, first : first + 1] * everyone[0].astype(f32)
        for n in range(1, members):
            others = others + coef[:, first + n : first + n + 1] * everyone[n].astype(f32)
        toward = (chosen - target_held[...]) * (1.0 / (members * dist[:, pairs + a : pairs + a + 1]))
        shown[a] = (toward - (reach * chosen - others) * (1.0 / (members * (members - 1)))).astype(bf16)
        copies.append(pltpu.make_async_copy(shown.at[a], grads.at[a], shown_sems.at[a]))
        copies[-1].start()
    total = jnp.dot(shown[0], hidden[0], preferred_element_type=f32)
    for a in range(1, held):
        total = total + jnp.dot(shown[a], hidden[a], preferred_element_type=f32)
    tall = jnp.concatenate([total, jnp.zeros((ACROSS - total.shape[0], total.shape[1]), f32)], axis=0)
    tall_held[...] = tall.T
    parts_held[...] = packed(tall_held).astype(bf16).reshape(parts_held.shape)
    pieces = min(parts_sems.shape[0], parts_held.shape[0])
    step = parts_held.shape[0] // pieces
    for index in range(pieces):
        part = slice(index * step, (index + 1) * step)
        copy = pltpu.make_async_copy(parts_held.at[part], weight_grad.at[part], parts_sems.at[index])
        copy.start()
        copies.append(copy)
    for copy in copies:
        copy.wait()


def backward(place, grads, w_out, slope, neighbours, weight, below, middle, above, w_rows):
    held, nodes, width = middle.shape
    variables = w_out.shape[0]
    w_rows[64:ROWS] = jnp.zeros((ROWS - 64, width), f32)
    w_rows[0:variables] = w_out[...].astype(f32)
    rows = w_rows[...].astype(bf16)
    first = (place[0] - 1) * nodes
    slots = neighbours.shape[1]
    step = 128
    spread = mixing(neighbours[...], weight[...], first, 3 * nodes).astype(bf16)
    for m in range(held):
        total = None
        lines = grads[m].astype(f32).T.astype(bf16)
        for start in range(0, slots, step):
            part = slice(start, start + step)
            back = jnp.dot(lines[part], rows, preferred_element_type=f32)
            grad_pre = (back * slope[m, part].astype(f32)).astype(bf16)
            term = jnp.dot(spread[:, part], grad_pre, preferred_element_type=f32)
            total = term if total is None else total + term
        below[m] = total[:nodes].astype(bf16)
        middle[m] = total[nodes : 2 * nodes]
        above[m] = total[2 * nodes :].astype(bf16)


def node_grads(middle, from_above, from_below, w_in, out):
    members, nodes, _ = out.shape
    total = middle[...] + from_above[...].astype(f32) + from_below[...].astype(f32)
    total = total.astype(bf16).reshape(members * nodes, -1)
    done = lax.dot_general(total, w_in[...], NT, preferred_element_type=f32)
    out[...] = done.astype(bf16).reshape(out.shape)


def gathered_sum(parts, share, out):
    total = jnp.sum(parts[...].astype(f32), axis=0)
    lane = lax.broadcasted_iota(jnp.int32, total.shape, 1)
    total = jnp.where(lane == total.shape[1] - 1, share[0:1, 0:1], total)
    out[...] = jnp.broadcast_to(total[None], out.shape)


def last_sum(parts, weight_grad, score):
    total = parts[0]
    for k in range(1, parts.shape[0]):
        total = total + parts[k]
    half = ACROSS // 2
    over = weight_grad.shape[1] - half
    for row in range(total.shape[0]):
        for k in range(QUAD):
            first, last = k * half, 2 * ACROSS + k * (ROWS - half)
            weight_grad[row * QUAD + k : row * QUAD + k + 1, :half] = total[row : row + 1, first : first + half]
            weight_grad[row * QUAD + k : row * QUAD + k + 1, half:] = total[row : row + 1, last : last + over]
    score[...] = total[0:1, 3 * ACROSS - 1 :]


def per_device(latent, edge_weight, neighbours, band_rows, w_in, w_out, target):
    members_dev, nodes, width = latent.shape
    slots = edge_weight.shape[1]
    variables = w_out.shape[0]
    groups, bands = lax.axis_size("member"), lax.axis_size("space")
    members = groups * members_dev
    band = lax.axis_index("space").astype(jnp.int32)
    group = lax.axis_index("member").astype(jnp.int32)
    up = [(i, i + 1) for i in range(bands - 1)]
    down = [(i + 1, i) for i in range(bands - 1)]
    before = lax.ppermute(latent, "space", up)
    after = lax.ppermute(latent, "space", down)
    where = band.reshape(1)
    mine_at = (group * members_dev).reshape(1)

    shape = jax.ShapeDtypeStruct
    big = (members_dev, slots, width)
    decoded = (members_dev, ROWS, slots)
    kept = (members_dev, 6 * nodes, width)

    def stay(array):
        return pltpu.with_memory_space_constraint(array, pltpu.HBM)

    weights, rows, spread, mine = call(
        prepare,
        (
            pltpu.VMEM(w_in.shape, bf16), pltpu.VMEM((ROWS, width), bf16),
            pltpu.VMEM((slots, 6 * nodes), bf16), pltpu.VMEM((members_dev * nodes, width), f32),
        ),
        [SMEM, VMEM, HBM] + [VMEM] * 3,
        (VMEM,) * 4,
        [pltpu.VMEM((ROWS, width), f32), pltpu.SemaphoreType.DMA((4,))],
        flops=1 << 28, moved=4 << 20,
    )(where, stay(latent), stay(w_in), stay(w_out), stay(neighbours), stay(edge_weight))
    sent, projected = call(
        forward,
        (pltpu.HBM((groups, *decoded), bf16), pltpu.HBM(kept, bf16)),
        [SMEM] + [VMEM] * 6,
        (HBM, HBM),
        [
            pltpu.VMEM((2 * members_dev * nodes, width), bf16),
            pltpu.VMEM(kept, bf16),
            pltpu.VMEM(decoded, bf16),
            pltpu.SemaphoreType.DMA((members_dev,)),
            pltpu.SemaphoreType.DMA((members_dev, groups)),
        ],
        flops=1 << 30, moved=8 << 20,
    )(band_rows, before, mine, after, weights, rows, spread)

    everyone = lax.all_to_all(sent, "member", 0, 0, tiled=True).reshape(members, ROWS, slots)
    hidden, slope, done = call(
        activations,
        (pltpu.VMEM(big, bf16), pltpu.HBM(big, bf16), shape((8, 128), f32)),
        [SMEM] + [VMEM] * 3,
        (VMEM, HBM, VMEM),
        [pltpu.VMEM(big, bf16), pltpu.SemaphoreType.DMA((members_dev, slots // 128))],
        flops=1 << 30, moved=8 << 20,
    )(where, stay(projected), stay(neighbours), stay(edge_weight))

    def distances_body(*refs):
        distances(members_dev, *refs)

    sums = call(
        distances_body, shape((bands, 128), f32), [SMEM, SMEM, VMEM, VMEM, HBM], VMEM,
        [pltpu.VMEM((ROWS, slots), f32)], flops=1 << 22, moved=2 << 20,
    )(mine_at, band_rows, everyone, target, done)
    sums = lax.all_to_all(sums, "space", 0, 0, tiled=True)

    columns = width // bands
    tiles = (bands, columns // QUAD, 3 * ACROSS)

    def grads_body(*refs):
        output_grads(variables, *refs)

    grads, weight_parts, share = call(
        grads_body,
        (pltpu.HBM(decoded, bf16), pltpu.HBM(tiles, bf16), shape((8, 128), f32)),
        [SMEM, SMEM, VMEM, VMEM, VMEM, VMEM],
        (HBM, HBM, VMEM),
        [
            pltpu.VMEM((ROWS, slots), f32),
            pltpu.VMEM(decoded, bf16),
            pltpu.VMEM((width, ACROSS), f32),
            pltpu.VMEM(tiles, bf16),
            pltpu.SemaphoreType.DMA((members_dev,)),
            pltpu.SemaphoreType.DMA((4,)),
        ],
        flops=1 << 28, moved=4 << 20,
    )(mine_at, band_rows, sums, everyone, target, hidden)
    weight_parts = lax.all_to_all(weight_parts, "space", 0, 0, tiled=True)

    small = (members_dev, nodes, width)
    lower, middle, upper = call(
        backward,
        (pltpu.VMEM(small, bf16), pltpu.VMEM(small, f32), pltpu.VMEM(small, bf16)),
        [SMEM] + [VMEM] * 5,
        (VMEM,) * 3,
        [pltpu.VMEM((ROWS, width), f32)],
        flops=1 << 29, moved=4 << 20,
    )(where, stay(grads), stay(w_out), stay(slope), stay(neighbours), stay(edge_weight))
    from_above = lax.ppermute(lower, "space", down)
    from_below = lax.ppermute(upper, "space", up)
    grad_latent = call(
        node_grads, shape(small, bf16), [VMEM] * 4, VMEM, flops=1 << 28, moved=4 << 20
    )(middle, from_above, from_below, w_in)

    total = call(
        gathered_sum, shape((groups, *tiles[1:]), f32), [VMEM] * 2, VMEM, flops=1 << 18, moved=1 << 18
    )(weight_parts, share)
    total = lax.all_to_all(total, "member", 0, 0, tiled=True)
    grad_w_out, score = call(
        last_sum, (shape((columns, variables), f32), shape((1, 1), f32)), [VMEM], (VMEM, VMEM),
        flops=1 << 16, moved=1 << 16,
    )(total)
    return (score.reshape(()), grad_latent, grad_w_out.T)


def solution(mesh):
    return jax.shard_map(
        per_device,
        mesh=mesh,
        in_specs=(
            P("member", "space", None),
            P(None, "space"),
            P(None, "space"),
            P("space"),
            P(),
            P(),
            P(None, "space"),
        ),
        out_specs=(P(), P("member", "space", None), P(None, "space")),
        check_vma=False,
    )
```

```python
import jax
import jax.numpy as jnp
from jax import lax
from jax.experimental import pallas as pl
from jax.experimental.pallas import tpu as pltpu
from jax.sharding import PartitionSpec as P

epsilon = 1e-06
f32 = jnp.float32
bf16 = jnp.bfloat16
VMEM = pl.BlockSpec(memory_space=pltpu.VMEM)
SMEM = pl.BlockSpec(memory_space=pltpu.SMEM)
NT = (((1,), (1,)), ((), ()))
ROWS = 72
ACROSS = 128
QUAD = 4


HBM = pl.BlockSpec(memory_space=pltpu.HBM)


def call(body, outs, specs, out_specs, scratch=(), room=24 << 10, flops=0, moved=0):
    return pl.pallas_call(
        body,
        out_shape=outs,
        in_specs=specs,
        out_specs=out_specs,
        scratch_shapes=scratch,
        compiler_params=pltpu.CompilerParams(vmem_limit_bytes=room << 10),
        cost_estimate=pl.CostEstimate(flops=flops, bytes_accessed=moved, transcendentals=0),
    )


def mixing(neighbours, weight, first_node, rows):
    node = lax.broadcasted_iota(jnp.int32, (rows, neighbours.shape[1]), 0) + first_node
    total = jnp.where(node == neighbours[0:1], weight[0:1], 0.0)
    for k in range(1, neighbours.shape[0]):
        total = total + jnp.where(node == neighbours[k : k + 1], weight[k : k + 1], 0.0)
    return total


def prepare(place, own, w_in, w_out, neighbours, weight, weights, rows, spread, mine, w_held, w_sems):
    loads = []
    pieces = w_sems.shape[0]
    step = weights.shape[0] // pieces
    for index in range(pieces):
        part = slice(index * step, (index + 1) * step)
        loads.append(pltpu.make_async_copy(w_in.at[part], weights.at[part], w_sems.at[index]))
        loads[-1].start()
    nodes = spread.shape[1] // 6
    mixed = mixing(neighbours[...], weight[...], (place[0] - 1) * nodes, 3 * nodes)
    spread[...] = jnp.concatenate([mixed, mixed], axis=0).T.astype(bf16)
    w_held[64:ROWS] = jnp.zeros((ROWS - 64, w_held.shape[1]), f32)
    w_held[0 : w_out.shape[0]] = w_out[...].astype(f32)
    rows[...] = w_held[...].astype(bf16)
    for load in loads:
        load.wait()
    here = own[...].reshape(mine.shape)
    mine[...] = jnp.dot(here, weights[...], preferred_element_type=f32)


def forward(
    rows_here, before, mine, after, weights, rows, spread,
    sent, projected,
    latents, held, decoded, held_sems, sent_sems,
):
    members, nodes, _ = before.shape
    slots = spread.shape[0]
    step = 512
    around = 3 * nodes
    both = members * nodes
    latents[:both] = before[...].reshape(both, -1)
    latents[both:] = after[...].reshape(both, -1)
    whole = jnp.dot(latents[...], weights[...], preferred_element_type=f32)
    for k, source in enumerate((whole[:both], mine[...], whole[both:])):
        high = source.astype(bf16)
        low = (source - high.astype(f32)).astype(bf16)
        for m in range(members):
            first = k * nodes
            held[m, first : first + nodes] = high[m * nodes : (m + 1) * nodes]
            held[m, around + first : around + first + nodes] = low[m * nodes : (m + 1) * nodes]
    copies = []
    for m in range(members):
        copies.append(pltpu.make_async_copy(held.at[m], projected.at[m], held_sems.at[m]))
        copies[-1].start()
    slot = lax.broadcasted_iota(jnp.int32, (ROWS, step), 1)
    for m in range(members):
        for start in range(0, slots, step):
            part = slice(start, start + step)
            preact = jnp.dot(spread[part], held[m], preferred_element_type=f32)
            out = (preact * (0.5 * jnp.tanh(0.5 * preact) + 0.5)).astype(bf16)
            fields = lax.dot_general(rows[...], out, NT, preferred_element_type=f32)
            decoded[m, :, part] = jnp.where(slot + start < rows_here[0], fields, 0.0).astype(bf16)
        for k in range(sent.shape[0]):
            copies.append(pltpu.make_async_copy(decoded.at[m], sent.at[k, m], sent_sems.at[m, k]))
            copies[-1].start()
    for copy in copies:
        copy.wait()


def activations(place, projected, neighbours, weight, hidden, slope, done, held, sems):
    done[...] = jnp.zeros_like(done)
    members = projected.shape[0]
    slots = neighbours.shape[1]
    step = 128
    nodes = projected.shape[1] // 6
    spread = mixing(neighbours[...], weight[...], (place[0] - 1) * nodes, 3 * nodes)
    spread = jnp.concatenate([spread, spread], axis=0).T.astype(bf16)
    copies = []
    for m in range(members):
        for index, start in enumerate(range(0, slots, step)):
            part = slice(start, start + step)
            preact = jnp.dot(spread[part], projected[m], preferred_element_type=f32)
            gate = 0.5 * jnp.tanh(0.5 * preact) + 0.5
            lit = preact * gate
            hidden[m, part] = lit.astype(bf16)
            held[m, part] = (gate + lit * (1.0 - gate)).astype(bf16)
            copies.append(pltpu.make_async_copy(held.at[m, part], slope.at[m, part], sems.at[m, index]))
            copies[-1].start()
    for copy in copies:
        copy.wait()


def lanes_of(squares):
    rows, slots = squares.shape
    tall = jnp.sum(squares.reshape(rows // 8, 8, slots), axis=0)
    total = tall[:, 0:128]
    for start in range(128, slots, 128):
        total = total + tall[:, start : start + 128]
    return jnp.sum(total, axis=0, keepdims=True)


def masked_target(rows_here, target, held):
    slot = lax.broadcasted_iota(jnp.int32, target.shape, 1)
    held[64:ROWS] = jnp.zeros((ROWS - 64, target.shape[1]), f32)
    held[0 : target.shape[0]] = jnp.where(slot < rows_here[0], target[...], 0.0)


def distances(owned, place, rows_here, everyone, target, done, sums, target_held):
    members = everyone.shape[0]
    masked_target(rows_here, target, target_held)
    lines = []
    for a in range(owned):
        own = everyone[place[0] + a].astype(f32)
        for n in range(members):
            gap = own - everyone[n].astype(f32)
            lines.append(lanes_of(gap * gap))
    for a in range(owned):
        gap = everyone[place[0] + a].astype(f32) - target_held[...]
        lines.append(lanes_of(gap * gap))
    lines.append(jnp.zeros((128 - len(lines), 128), f32))
    table = jnp.concatenate(lines, axis=0).T
    line = jnp.sum(table, axis=0, keepdims=True)
    lane = lax.broadcasted_iota(jnp.int32, (1, 128), 1)
    line = jnp.where(lane == 127, rows_here[0].astype(f32), line)
    sums[...] = jnp.broadcast_to(line, sums.shape)


def packed(tall):
    rows = tall.shape[0] // QUAD
    column = [tall[pl.ds(k, rows, stride=QUAD), :] for k in range(QUAD)]
    lane = lax.broadcasted_iota(jnp.int32, (rows, ACROSS), 1)
    half = ACROSS // 2
    over = ROWS - half
    rest = pltpu.roll(column[0], half, 1)
    for k in range(1, QUAD):
        rest = jnp.where(lane < k * over, rest, pltpu.roll(column[k], half + k * over, 1))
    return jnp.concatenate(
        [
            jnp.where(lane < half, column[0], pltpu.roll(column[1], half, 1)),
            jnp.where(lane < half, column[2], pltpu.roll(column[3], half, 1)),
            rest,
        ],
        axis=1,
    )


def output_grads(
    variables, place, rows_here, sums, everyone, target, hidden,
    grads, weight_grad, share,
    target_held, shown, tall_held, parts_held, shown_sems, parts_sems,
):
    members = everyone.shape[0]
    held = grads.shape[0]
    masked_target(rows_here, target, target_held)
    line = jnp.sum(sums[...], axis=0, keepdims=True)
    lane = lax.broadcasted_iota(jnp.int32, (1, 128), 1)
    cells = variables * line[:, 127:128]
    dist = jnp.sqrt(line / cells + epsilon)
    pairs = held * members
    apart = lane < pairs
    for a in range(held):
        apart = apart & (lane != a * members + place[0] + a)
    coef = jnp.where(apart, 1.0 / dist, 0.0)
    per_target = (lane >= pairs) & (lane < pairs + held)
    share[...] = jnp.sum(
        jnp.where(per_target, dist / members, 0.0)
        - jnp.where(apart, dist / (2.0 * members * (members - 1)), 0.0),
        axis=1, keepdims=True,
    ) + jnp.zeros(share.shape, f32)
    copies = []
    for a in range(held):
        chosen = everyone[place[0] + a].astype(f32)
        first = a * members
        reach = jnp.sum(jnp.where((lane >= first) & (lane < first + members), coef, 0.0), axis=1, keepdims=True)
        others = coef[:, first : first + 1] * everyone[0].astype(f32)
        for n in range(1, members):
            others = others + coef[:, first + n : first + n + 1] * everyone[n].astype(f32)
        toward = (chosen - target_held[...]) * (1.0 / (members * dist[:, pairs + a : pairs + a + 1]))
        shown[a] = (toward - (reach * chosen - others) * (1.0 / (members * (members - 1)))).astype(bf16)
        copies.append(pltpu.make_async_copy(shown.at[a], grads.at[a], shown_sems.at[a]))
        copies[-1].start()
    total = jnp.dot(shown[0], hidden[0], preferred_element_type=f32)
    for a in range(1, held):
        total = total + jnp.dot(shown[a], hidden[a], preferred_element_type=f32)
    tall = jnp.concatenate([total, jnp.zeros((ACROSS - total.shape[0], total.shape[1]), f32)], axis=0)
    tall_held[...] = tall.T
    parts_held[...] = packed(tall_held).astype(bf16).reshape(parts_held.shape)
    pieces = min(parts_sems.shape[0], parts_held.shape[0])
    step = parts_held.shape[0] // pieces
    for index in range(pieces):
        part = slice(index * step, (index + 1) * step)
        copy = pltpu.make_async_copy(parts_held.at[part], weight_grad.at[part], parts_sems.at[index])
        copy.start()
        copies.append(copy)
    for copy in copies:
        copy.wait()


def backward(place, grads, w_out, slope, neighbours, weight, below, middle, above, w_rows):
    held, nodes, width = middle.shape
    variables = w_out.shape[0]
    w_rows[64:ROWS] = jnp.zeros((ROWS - 64, width), f32)
    w_rows[0:variables] = w_out[...].astype(f32)
    rows = w_rows[...].astype(bf16)
    first = (place[0] - 1) * nodes
    slots = neighbours.shape[1]
    step = 128
    spread = mixing(neighbours[...], weight[...], first, 3 * nodes).astype(bf16)
    for m in range(held):
        total = None
        lines = grads[m].astype(f32).T.astype(bf16)
        for start in range(0, slots, step):
            part = slice(start, start + step)
            back = jnp.dot(lines[part], rows, preferred_element_type=f32)
            grad_pre = (back * slope[m, part].astype(f32)).astype(bf16)
            term = jnp.dot(spread[:, part], grad_pre, preferred_element_type=f32)
            total = term if total is None else total + term
        below[m] = total[:nodes].astype(bf16)
        middle[m] = total[nodes : 2 * nodes]
        above[m] = total[2 * nodes :].astype(bf16)


def node_grads(middle, from_above, from_below, w_in, out):
    members, nodes, _ = out.shape
    total = middle[...] + from_above[...].astype(f32) + from_below[...].astype(f32)
    total = total.astype(bf16).reshape(members * nodes, -1)
    done = lax.dot_general(total, w_in[...], NT, preferred_element_type=f32)
    out[...] = done.astype(bf16).reshape(out.shape)


def gathered_sum(parts, share, out):
    total = jnp.sum(parts[...].astype(f32), axis=0)
    lane = lax.broadcasted_iota(jnp.int32, total.shape, 1)
    total = jnp.where(lane == total.shape[1] - 1, share[0:1, 0:1], total)
    out[...] = jnp.broadcast_to(total[None], out.shape)


def last_sum(parts, weight_grad, score):
    total = parts[0]
    for k in range(1, parts.shape[0]):
        total = total + parts[k]
    half = ACROSS // 2
    over = weight_grad.shape[1] - half
    for row in range(total.shape[0]):
        for k in range(QUAD):
            first, last = k * half, 2 * ACROSS + k * (ROWS - half)
            weight_grad[row * QUAD + k : row * QUAD + k + 1, :half] = total[row : row + 1, first : first + half]
            weight_grad[row * QUAD + k : row * QUAD + k + 1, half:] = total[row : row + 1, last : last + over]
    score[...] = total[0:1, 3 * ACROSS - 1 :]


def per_device(latent, edge_weight, neighbours, band_rows, w_in, w_out, target):
    members_dev, nodes, width = latent.shape
    slots = edge_weight.shape[1]
    variables = w_out.shape[0]
    groups, bands = lax.axis_size("member"), lax.axis_size("space")
    members = groups * members_dev
    band = lax.axis_index("space").astype(jnp.int32)
    group = lax.axis_index("member").astype(jnp.int32)
    up = [(i, i + 1) for i in range(bands - 1)]
    down = [(i + 1, i) for i in range(bands - 1)]
    before = lax.ppermute(latent, "space", up)
    after = lax.ppermute(latent, "space", down)
    where = band.reshape(1)
    mine_at = (group * members_dev).reshape(1)

    shape = jax.ShapeDtypeStruct
    big = (members_dev, slots, width)
    decoded = (members_dev, ROWS, slots)
    kept = (members_dev, 6 * nodes, width)

    def stay(array):
        return pltpu.with_memory_space_constraint(array, pltpu.HBM)

    weights, rows, spread, mine = call(
        prepare,
        (
            pltpu.VMEM(w_in.shape, bf16), pltpu.VMEM((ROWS, width), bf16),
            pltpu.VMEM((slots, 6 * nodes), bf16), pltpu.VMEM((members_dev * nodes, width), f32),
        ),
        [SMEM, VMEM, HBM] + [VMEM] * 3,
        (VMEM,) * 4,
        [pltpu.VMEM((ROWS, width), f32), pltpu.SemaphoreType.DMA((4,))],
        flops=1 << 28, moved=4 << 20,
    )(where, stay(latent), stay(w_in), stay(w_out), stay(neighbours), stay(edge_weight))
    sent, projected = call(
        forward,
        (pltpu.HBM((groups, *decoded), bf16), pltpu.HBM(kept, bf16)),
        [SMEM] + [VMEM] * 6,
        (HBM, HBM),
        [
            pltpu.VMEM((2 * members_dev * nodes, width), bf16),
            pltpu.VMEM(kept, bf16),
            pltpu.VMEM(decoded, bf16),
            pltpu.SemaphoreType.DMA((members_dev,)),
            pltpu.SemaphoreType.DMA((members_dev, groups)),
        ],
        flops=1 << 30, moved=8 << 20,
    )(band_rows, before, mine, after, weights, rows, spread)

    everyone = lax.all_to_all(sent, "member", 0, 0, tiled=True).reshape(members, ROWS, slots)
    hidden, slope, done = call(
        activations,
        (pltpu.VMEM(big, bf16), pltpu.HBM(big, bf16), shape((8, 128), f32)),
        [SMEM] + [VMEM] * 3,
        (VMEM, HBM, VMEM),
        [pltpu.VMEM(big, bf16), pltpu.SemaphoreType.DMA((members_dev, slots // 128))],
        flops=1 << 30, moved=8 << 20,
    )(where, stay(projected), stay(neighbours), stay(edge_weight))

    def distances_body(*refs):
        distances(members_dev, *refs)

    sums = call(
        distances_body, shape((bands, 128), f32), [SMEM, SMEM, VMEM, VMEM, HBM], VMEM,
        [pltpu.VMEM((ROWS, slots), f32)], flops=1 << 22, moved=2 << 20,
    )(mine_at, band_rows, everyone, target, done)
    sums = lax.all_to_all(sums, "space", 0, 0, tiled=True)

    columns = width // bands
    tiles = (bands, columns // QUAD, 3 * ACROSS)

    def grads_body(*refs):
        output_grads(variables, *refs)

    grads, weight_parts, share = call(
        grads_body,
        (pltpu.HBM(decoded, bf16), pltpu.HBM(tiles, bf16), shape((8, 128), f32)),
        [SMEM, SMEM, VMEM, VMEM, VMEM, VMEM],
        (HBM, HBM, VMEM),
        [
            pltpu.VMEM((ROWS, slots), f32),
            pltpu.VMEM(decoded, bf16),
            pltpu.VMEM((width, ACROSS), f32),
            pltpu.VMEM(tiles, bf16),
            pltpu.SemaphoreType.DMA((members_dev,)),
            pltpu.SemaphoreType.DMA((4,)),
        ],
        flops=1 << 28, moved=4 << 20,
    )(mine_at, band_rows, sums, everyone, target, hidden)
    weight_parts = lax.all_to_all(weight_parts, "space", 0, 0, tiled=True)

    small = (members_dev, nodes, width)
    lower, middle, upper = call(
        backward,
        (pltpu.VMEM(small, bf16), pltpu.VMEM(small, f32), pltpu.VMEM(small, bf16)),
        [SMEM] + [VMEM] * 5,
        (VMEM,) * 3,
        [pltpu.VMEM((ROWS, width), f32)],
        flops=1 << 29, moved=4 << 20,
    )(where, stay(grads), stay(w_out), stay(slope), stay(neighbours), stay(edge_weight))
    from_above = lax.ppermute(lower, "space", down)
    from_below = lax.ppermute(upper, "space", up)
    grad_latent = call(
        node_grads, shape(small, bf16), [VMEM] * 4, VMEM, flops=1 << 28, moved=4 << 20
    )(middle, from_above, from_below, w_in)

    total = call(
        gathered_sum, shape((groups, *tiles[1:]), f32), [VMEM] * 2, VMEM, flops=1 << 18, moved=1 << 18
    )(weight_parts, share)
    total = lax.all_to_all(total, "member", 0, 0, tiled=True)
    grad_w_out, score = call(
        last_sum, (shape((columns, variables), f32), shape((1, 1), f32)), [VMEM], (VMEM, VMEM),
        flops=1 << 16, moved=1 << 16,
    )(total)
    return (score.reshape(()), grad_latent, grad_w_out.T)


def solution(mesh):
    return jax.shard_map(
        per_device,
        mesh=mesh,
        in_specs=(
            P("member", "space", None),
            P(None, "space"),
            P(None, "space"),
            P("space"),
            P(),
            P(),
            P(None, "space"),
        ),
        out_specs=(P(), P("member", "space", None), P(None, "space")),
        check_vma=False,
    )
```

```python
import jax
import jax.numpy as jnp
from jax import lax
from jax.experimental import pallas as pl
from jax.experimental.pallas import tpu as pltpu
from jax.sharding import PartitionSpec as P

epsilon = 1e-06
f32 = jnp.float32
bf16 = jnp.bfloat16
VMEM = pl.BlockSpec(memory_space=pltpu.VMEM)
SMEM = pl.BlockSpec(memory_space=pltpu.SMEM)
NT = (((1,), (1,)), ((), ()))
ROWS = 72
ACROSS = 128
QUAD = 4


HBM = pl.BlockSpec(memory_space=pltpu.HBM)


def call(body, outs, specs, out_specs, scratch=(), room=24 << 10, flops=0, moved=0):
    return pl.pallas_call(
        body,
        out_shape=outs,
        in_specs=specs,
        out_specs=out_specs,
        scratch_shapes=scratch,
        compiler_params=pltpu.CompilerParams(vmem_limit_bytes=room << 10),
        cost_estimate=pl.CostEstimate(flops=flops, bytes_accessed=moved, transcendentals=0),
    )


def mixing(neighbours, weight, bands, nodes):
    row = lax.broadcasted_iota(jnp.int32, (len(bands) * nodes, neighbours.shape[1]), 0)
    node = row + bands[0] * nodes
    for k in range(1, len(bands)):
        node = jnp.where(row >= k * nodes, row + (bands[k] - k) * nodes, node)
    total = jnp.where(node == neighbours[0:1], weight[0:1], 0.0)
    for k in range(1, neighbours.shape[0]):
        total = total + jnp.where(node == neighbours[k : k + 1], weight[k : k + 1], 0.0)
    return total


def paired(band):
    side = 1 - 2 * lax.rem(band, 2)
    return band + side, band, band - side


def prepare(place, own, w_in, w_out, neighbours, weight, weights, rows, spread, mine, w_held, w_sems):
    loads = []
    pieces = w_sems.shape[0]
    step = weights.shape[0] // pieces
    for index in range(pieces):
        part = slice(index * step, (index + 1) * step)
        loads.append(pltpu.make_async_copy(w_in.at[part], weights.at[part], w_sems.at[index]))
        loads[-1].start()
    nodes = spread.shape[1] // 6
    mixed = mixing(neighbours[...], weight[...], paired(place[0]), nodes)
    spread[...] = jnp.concatenate([mixed, mixed], axis=0).T.astype(bf16)
    w_held[64:ROWS] = jnp.zeros((ROWS - 64, w_held.shape[1]), f32)
    w_held[0 : w_out.shape[0]] = w_out[...].astype(f32)
    rows[...] = w_held[...].astype(bf16)
    for load in loads:
        load.wait()
    here = own[...].reshape(mine.shape)
    mine[...] = jnp.dot(here, weights[...], preferred_element_type=f32)


def forward(
    rows_here, near, mine, far, weights, rows, spread,
    sent, projected,
    latents, held, decoded, held_sems, sent_sems,
):
    members, nodes, _ = near.shape
    slots = spread.shape[0]
    step = 512
    around = 3 * nodes
    both = members * nodes
    latents[:both] = near[...].reshape(both, -1)
    latents[both:] = far[...].reshape(both, -1)
    whole = jnp.dot(latents[...], weights[...], preferred_element_type=f32)
    for k, source in enumerate((whole[:both], mine[...], whole[both:])):
        high = source.astype(bf16)
        low = (source - high.astype(f32)).astype(bf16)
        for m in range(members):
            first = k * nodes
            held[m, first : first + nodes] = high[m * nodes : (m + 1) * nodes]
            held[m, around + first : around + first + nodes] = low[m * nodes : (m + 1) * nodes]
    copies = []
    for m in range(members):
        copies.append(pltpu.make_async_copy(held.at[m], projected.at[m], held_sems.at[m]))
        copies[-1].start()
    slot = lax.broadcasted_iota(jnp.int32, (ROWS, step), 1)
    for m in range(members):
        for start in range(0, slots, step):
            part = slice(start, start + step)
            preact = jnp.dot(spread[part], held[m], preferred_element_type=f32)
            out = (preact * (0.5 * jnp.tanh(0.5 * preact) + 0.5)).astype(bf16)
            fields = lax.dot_general(rows[...], out, NT, preferred_element_type=f32)
            decoded[m, :, part] = jnp.where(slot + start < rows_here[0], fields, 0.0).astype(bf16)
        for k in range(sent.shape[0]):
            copies.append(pltpu.make_async_copy(decoded.at[m], sent.at[k, m], sent_sems.at[m, k]))
            copies[-1].start()
    for copy in copies:
        copy.wait()


def activations(place, projected, neighbours, weight, hidden, slope, done, held, sems):
    done[...] = jnp.zeros_like(done)
    members = projected.shape[0]
    slots = neighbours.shape[1]
    step = 128
    nodes = projected.shape[1] // 6
    spread = mixing(neighbours[...], weight[...], paired(place[0]), nodes)
    spread = jnp.concatenate([spread, spread], axis=0).T.astype(bf16)
    copies = []
    for m in range(members):
        for index, start in enumerate(range(0, slots, step)):
            part = slice(start, start + step)
            preact = jnp.dot(spread[part], projected[m], preferred_element_type=f32)
            gate = 0.5 * jnp.tanh(0.5 * preact) + 0.5
            lit = preact * gate
            hidden[m, part] = lit.astype(bf16)
            held[m, part] = (gate + lit * (1.0 - gate)).astype(bf16)
            copies.append(pltpu.make_async_copy(held.at[m, part], slope.at[m, part], sems.at[m, index]))
            copies[-1].start()
    for copy in copies:
        copy.wait()


def lanes_of(squares):
    rows, slots = squares.shape
    tall = jnp.sum(squares.reshape(rows // 8, 8, slots), axis=0)
    total = tall[:, 0:128]
    for start in range(128, slots, 128):
        total = total + tall[:, start : start + 128]
    return jnp.sum(total, axis=0, keepdims=True)


def masked_target(rows_here, target, held):
    slot = lax.broadcasted_iota(jnp.int32, target.shape, 1)
    held[64:ROWS] = jnp.zeros((ROWS - 64, target.shape[1]), f32)
    held[0 : target.shape[0]] = jnp.where(slot < rows_here[0], target[...], 0.0)


def distances(owned, place, rows_here, everyone, target, done, sums, target_held):
    members = everyone.shape[0]
    masked_target(rows_here, target, target_held)
    lines = []
    for a in range(owned):
        own = everyone[place[0] + a].astype(f32)
        for n in range(members):
            gap = own - everyone[n].astype(f32)
            lines.append(lanes_of(gap * gap))
    for a in range(owned):
        gap = everyone[place[0] + a].astype(f32) - target_held[...]
        lines.append(lanes_of(gap * gap))
    lines.append(jnp.zeros((128 - len(lines), 128), f32))
    table = jnp.concatenate(lines, axis=0).T
    line = jnp.sum(table, axis=0, keepdims=True)
    lane = lax.broadcasted_iota(jnp.int32, (1, 128), 1)
    line = jnp.where(lane == 127, rows_here[0].astype(f32), line)
    sums[...] = jnp.broadcast_to(line, sums.shape)


def packed(tall):
    rows = tall.shape[0] // QUAD
    column = [tall[pl.ds(k, rows, stride=QUAD), :] for k in range(QUAD)]
    lane = lax.broadcasted_iota(jnp.int32, (rows, ACROSS), 1)
    half = ACROSS // 2
    over = ROWS - half
    rest = pltpu.roll(column[0], half, 1)
    for k in range(1, QUAD):
        rest = jnp.where(lane < k * over, rest, pltpu.roll(column[k], half + k * over, 1))
    return jnp.concatenate(
        [
            jnp.where(lane < half, column[0], pltpu.roll(column[1], half, 1)),
            jnp.where(lane < half, column[2], pltpu.roll(column[3], half, 1)),
            rest,
        ],
        axis=1,
    )


def output_grads(
    variables, place, rows_here, sums, everyone, target, hidden,
    grads, weight_grad, share,
    target_held, shown, tall_held, parts_held, shown_sems, parts_sems,
):
    members = everyone.shape[0]
    held = grads.shape[0]
    masked_target(rows_here, target, target_held)
    line = jnp.sum(sums[...], axis=0, keepdims=True)
    lane = lax.broadcasted_iota(jnp.int32, (1, 128), 1)
    cells = variables * line[:, 127:128]
    dist = jnp.sqrt(line / cells + epsilon)
    pairs = held * members
    apart = lane < pairs
    for a in range(held):
        apart = apart & (lane != a * members + place[0] + a)
    coef = jnp.where(apart, 1.0 / dist, 0.0)
    per_target = (lane >= pairs) & (lane < pairs + held)
    share[...] = jnp.sum(
        jnp.where(per_target, dist / members, 0.0)
        - jnp.where(apart, dist / (2.0 * members * (members - 1)), 0.0),
        axis=1, keepdims=True,
    ) + jnp.zeros(share.shape, f32)
    copies = []
    for a in range(held):
        chosen = everyone[place[0] + a].astype(f32)
        first = a * members
        reach = jnp.sum(jnp.where((lane >= first) & (lane < first + members), coef, 0.0), axis=1, keepdims=True)
        others = coef[:, first : first + 1] * everyone[0].astype(f32)
        for n in range(1, members):
            others = others + coef[:, first + n : first + n + 1] * everyone[n].astype(f32)
        toward = (chosen - target_held[...]) * (1.0 / (members * dist[:, pairs + a : pairs + a + 1]))
        shown[a] = (toward - (reach * chosen - others) * (1.0 / (members * (members - 1)))).astype(bf16)
        copies.append(pltpu.make_async_copy(shown.at[a], grads.at[a], shown_sems.at[a]))
        copies[-1].start()
    total = jnp.dot(shown[0], hidden[0], preferred_element_type=f32)
    for a in range(1, held):
        total = total + jnp.dot(shown[a], hidden[a], preferred_element_type=f32)
    tall = jnp.concatenate([total, jnp.zeros((ACROSS - total.shape[0], total.shape[1]), f32)], axis=0)
    tall_held[...] = tall.T
    parts_held[...] = packed(tall_held).astype(bf16).reshape(parts_held.shape)
    pieces = min(parts_sems.shape[0], parts_held.shape[0])
    step = parts_held.shape[0] // pieces
    for index in range(pieces):
        part = slice(index * step, (index + 1) * step)
        copy = pltpu.make_async_copy(parts_held.at[part], weight_grad.at[part], parts_sems.at[index])
        copy.start()
        copies.append(copy)
    for copy in copies:
        copy.wait()


def backward(place, grads, w_out, slope, neighbours, weight, below, middle, above, w_rows):
    held, nodes, width = middle.shape
    variables = w_out.shape[0]
    w_rows[64:ROWS] = jnp.zeros((ROWS - 64, width), f32)
    w_rows[0:variables] = w_out[...].astype(f32)
    rows = w_rows[...].astype(bf16)
    slots = neighbours.shape[1]
    step = 128
    band = place[0]
    spread = mixing(neighbours[...], weight[...], (band - 1, band, band + 1), nodes).astype(bf16)
    for m in range(held):
        total = None
        lines = grads[m].astype(f32).T.astype(bf16)
        for start in range(0, slots, step):
            part = slice(start, start + step)
            back = jnp.dot(lines[part], rows, preferred_element_type=f32)
            grad_pre = (back * slope[m, part].astype(f32)).astype(bf16)
            term = jnp.dot(spread[:, part], grad_pre, preferred_element_type=f32)
            total = term if total is None else total + term
        below[m] = total[:nodes].astype(bf16)
        middle[m] = total[nodes : 2 * nodes]
        above[m] = total[2 * nodes :].astype(bf16)


def node_grads(middle, from_above, from_below, w_in, out):
    members, nodes, _ = out.shape
    total = middle[...] + from_above[...].astype(f32) + from_below[...].astype(f32)
    total = total.astype(bf16).reshape(members * nodes, -1)
    done = lax.dot_general(total, w_in[...], NT, preferred_element_type=f32)
    out[...] = done.astype(bf16).reshape(out.shape)


def gathered_sum(parts, share, out):
    total = jnp.sum(parts[...].astype(f32), axis=0)
    lane = lax.broadcasted_iota(jnp.int32, total.shape, 1)
    total = jnp.where(lane == total.shape[1] - 1, share[0:1, 0:1], total)
    out[...] = jnp.broadcast_to(total[None], out.shape)


def last_sum(parts, weight_grad, score):
    total = parts[0]
    for k in range(1, parts.shape[0]):
        total = total + parts[k]
    half = ACROSS // 2
    over = weight_grad.shape[1] - half
    for row in range(total.shape[0]):
        for k in range(QUAD):
            first, last = k * half, 2 * ACROSS + k * (ROWS - half)
            weight_grad[row * QUAD + k : row * QUAD + k + 1, :half] = total[row : row + 1, first : first + half]
            weight_grad[row * QUAD + k : row * QUAD + k + 1, half:] = total[row : row + 1, last : last + over]
    score[...] = total[0:1, 3 * ACROSS - 1 :]


def per_device(latent, edge_weight, neighbours, band_rows, w_in, w_out, target):
    members_dev, nodes, width = latent.shape
    slots = edge_weight.shape[1]
    variables = w_out.shape[0]
    groups, bands = lax.axis_size("member"), lax.axis_size("space")
    members = groups * members_dev
    band = lax.axis_index("space").astype(jnp.int32)
    group = lax.axis_index("member").astype(jnp.int32)
    up = [(i, i + 1) for i in range(bands - 1)]
    down = [(i + 1, i) for i in range(bands - 1)]
    pairs = [(i, i + 1 - 2 * (i % 2)) for i in range(bands)]
    across = [(i, i - 1 + 2 * (i % 2)) for i in range(1, bands - 1)]
    near = lax.ppermute(latent, "space", pairs)
    far = lax.ppermute(latent, "space", across)
    where = band.reshape(1)
    mine_at = (group * members_dev).reshape(1)

    shape = jax.ShapeDtypeStruct
    big = (members_dev, slots, width)
    decoded = (members_dev, ROWS, slots)
    kept = (members_dev, 6 * nodes, width)

    def stay(array):
        return pltpu.with_memory_space_constraint(array, pltpu.HBM)

    weights, rows, spread, mine = call(
        prepare,
        (
            pltpu.VMEM(w_in.shape, bf16), pltpu.VMEM((ROWS, width), bf16),
            pltpu.VMEM((slots, 6 * nodes), bf16), pltpu.VMEM((members_dev * nodes, width), f32),
        ),
        [SMEM, VMEM, HBM] + [VMEM] * 3,
        (VMEM,) * 4,
        [pltpu.VMEM((ROWS, width), f32), pltpu.SemaphoreType.DMA((4,))],
        flops=1 << 28, moved=4 << 20,
    )(where, stay(latent), stay(w_in), stay(w_out), stay(neighbours), stay(edge_weight))
    sent, projected = call(
        forward,
        (pltpu.HBM((groups, *decoded), bf16), pltpu.HBM(kept, bf16)),
        [SMEM] + [VMEM] * 6,
        (HBM, HBM),
        [
            pltpu.VMEM((2 * members_dev * nodes, width), bf16),
            pltpu.VMEM(kept, bf16),
            pltpu.VMEM(decoded, bf16),
            pltpu.SemaphoreType.DMA((members_dev,)),
            pltpu.SemaphoreType.DMA((members_dev, groups)),
        ],
        flops=1 << 30, moved=8 << 20,
    )(band_rows, near, mine, far, weights, rows, spread)

    everyone = lax.all_to_all(sent, "member", 0, 0, tiled=True).reshape(members, ROWS, slots)
    hidden, slope, done = call(
        activations,
        (pltpu.VMEM(big, bf16), pltpu.HBM(big, bf16), shape((8, 128), f32)),
        [SMEM] + [VMEM] * 3,
        (VMEM, HBM, VMEM),
        [pltpu.VMEM(big, bf16), pltpu.SemaphoreType.DMA((members_dev, slots // 128))],
        flops=1 << 30, moved=8 << 20,
    )(where, stay(projected), stay(neighbours), stay(edge_weight))

    def distances_body(*refs):
        distances(members_dev, *refs)

    sums = call(
        distances_body, shape((bands, 128), f32), [SMEM, SMEM, VMEM, VMEM, HBM], VMEM,
        [pltpu.VMEM((ROWS, slots), f32)], flops=1 << 22, moved=2 << 20,
    )(mine_at, band_rows, everyone, target, done)
    sums = lax.all_to_all(sums, "space", 0, 0, tiled=True)

    columns = width // bands
    tiles = (bands, columns // QUAD, 3 * ACROSS)

    def grads_body(*refs):
        output_grads(variables, *refs)

    grads, weight_parts, share = call(
        grads_body,
        (pltpu.HBM(decoded, bf16), pltpu.HBM(tiles, bf16), shape((8, 128), f32)),
        [SMEM, SMEM, VMEM, VMEM, VMEM, VMEM],
        (HBM, HBM, VMEM),
        [
            pltpu.VMEM((ROWS, slots), f32),
            pltpu.VMEM(decoded, bf16),
            pltpu.VMEM((width, ACROSS), f32),
            pltpu.VMEM(tiles, bf16),
            pltpu.SemaphoreType.DMA((members_dev,)),
            pltpu.SemaphoreType.DMA((4,)),
        ],
        flops=1 << 28, moved=4 << 20,
    )(mine_at, band_rows, sums, everyone, target, hidden)
    weight_parts = lax.all_to_all(weight_parts, "space", 0, 0, tiled=True)

    small = (members_dev, nodes, width)
    lower, middle, upper = call(
        backward,
        (pltpu.VMEM(small, bf16), pltpu.VMEM(small, f32), pltpu.VMEM(small, bf16)),
        [SMEM] + [VMEM] * 5,
        (VMEM,) * 3,
        [pltpu.VMEM((ROWS, width), f32)],
        flops=1 << 29, moved=4 << 20,
    )(where, stay(grads), stay(w_out), stay(slope), stay(neighbours), stay(edge_weight))
    from_above = lax.ppermute(lower, "space", down)
    from_below = lax.ppermute(upper, "space", up)
    grad_latent = call(
        node_grads, shape(small, bf16), [VMEM] * 4, VMEM, flops=1 << 28, moved=4 << 20
    )(middle, from_above, from_below, w_in)

    total = call(
        gathered_sum, shape((groups, *tiles[1:]), f32), [VMEM] * 2, VMEM, flops=1 << 18, moved=1 << 18
    )(weight_parts, share)
    total = lax.all_to_all(total, "member", 0, 0, tiled=True)
    grad_w_out, score = call(
        last_sum, (shape((columns, variables), f32), shape((1, 1), f32)), [VMEM], (VMEM, VMEM),
        flops=1 << 16, moved=1 << 16,
    )(total)
    return (score.reshape(()), grad_latent, grad_w_out.T)


def solution(mesh):
    return jax.shard_map(
        per_device,
        mesh=mesh,
        in_specs=(
            P("member", "space", None),
            P(None, "space"),
            P(None, "space"),
            P("space"),
            P(),
            P(),
            P(None, "space"),
        ),
        out_specs=(P(), P("member", "space", None), P(None, "space")),
        check_vma=False,
    )
```
